32 devices in a mesh: ctx: 8 (over z, x), grp: 4 (over y, core).
Axes of the slice: x: 2, y: 2, z: 4, core: 2. Of those that a mesh axis runs over, the one named last changes fastest.
Arguments:
- queries: bfloat16 [4096, 1024], P(('grp', 'ctx')), parts along dimension 0, may hold values from -160 to 160
- key_states: bfloat16 [4096, 128], P(('grp', 'ctx')), parts along dimension 0, may hold values from -7 to 7
- value_states: bfloat16 [4096, 128], P(('grp', 'ctx')), parts along dimension 0, may hold values from -6 to 6
- out_grad: bfloat16 [4096, 1024], P(('grp', 'ctx')), parts along dimension 0, may hold values from -6 to 6
- doc_ids: int32 [4096], P('grp'), parts along dimension 0, may hold values from 0 to 15, never falling along the last dimension, each value on 1 to 128 neighbouring positions
Outputs:
- attn_out: bfloat16 [4096, 1024], P(('grp', 'ctx')), parts along dimension 0
- query_grad: bfloat16 [4096, 1024], P(('grp', 'ctx')), parts along dimension 0
- key_grad: float32 [4096, 128], P(('grp', 'ctx')), parts along dimension 0
- value_grad: float32 [4096, 128], P(('grp', 'ctx')), parts along dimension 0
The draws below stay inside these ranges and needn't reach their ends.
There are 4 independent parts, one for each index of `grp`. The reference program is written for one: setup_inputs(seed, part) draws one part's arguments, and reference() takes and returns one part's arrays. A program takes and returns all parts, laid end to end along the dimension named above; each array names one. Nothing has to cross between parts.
Inputs may be any that keep to these rules, and one draw needn't show every extreme that they name: `doc_ids`: nondecreasing along the sequence; each document covers 1 to 128 consecutive tokens, one exactly 128.
All inputs are finite; a program needn't handle non-finite values.
Results may differ from the reference program's by a relative error of at most 0.03.
Values may be sent and summed in bfloat16 or wider, within the bound.
A program may use at most 64 MiB of HBM per device.

```python
import math
import jax
import jax.numpy as jnp
import numpy as np
from jax import lax

H = 8
HD = 128
DOCS = 16
STRETCH = 64
SPAN = 2
TOKENS = 1024
MOST = 128
N_CTX = 8


def shared_keys(key):
    base = jnp.clip(jax.random.normal(jax.random.fold_in(key, 11), (TOKENS, HD), jnp.float32), -6.0, 6.0)
    return base


def draw_key_states(key, part):
    return shared_keys(key).astype(jnp.bfloat16)


def draw_queries(key, part):
    base = jnp.clip(jax.random.normal(jax.random.fold_in(key, 23), (TOKENS, H, HD), jnp.float32), -6.0, 6.0)
    return base.reshape(TOKENS, H * HD).astype(jnp.bfloat16)


def block_levels(own_key, dims, split, low, top_value):
    level, own = 1.0, jax.random.fold_in(own_key, 6)
    for axis_at, parts in split:
        steps = jnp.exp(jax.random.uniform(jax.random.fold_in(own, axis_at), (parts,), jnp.float32, low / len(split), top_value / len(split)))
        level = level * jnp.repeat(steps, dims[axis_at] // parts).reshape([-1 if axis == axis_at else 1 for axis in range(len(dims))])
    return level


def split_up(number_of, total, reach, lean):
    portions = [(1 << 20) // math.isqrt(rank ** lean) + 1 for rank in range(2, number_of + 1)]
    surplus, counts = total - reach - (number_of - 1), [1] * (number_of - 1)
    while surplus > 0:
        free = [i for i in range(number_of - 1) if counts[i] < reach]
        pool, remaining = sum([portions[i] for i in free]), surplus
        for i in free:
            extra = min(reach - counts[i], max(1, remaining * portions[i] // pool), surplus)
            counts[i] = counts[i] + extra
            surplus = surplus - extra
    return np.array([reach] + counts)


def ragged_sizes(stream_key, number_of, total, reach, lean):
    if number_of == 2:
        one = jax.random.randint(stream_key, (), max(1, total - reach), min(reach, total - 1) + 1)
        return jnp.stack([one, total - one])
    tallies = jnp.asarray(split_up(number_of, total, reach, lean), jnp.int32)
    couples = (number_of - 1) // 2
    source_of, receiver = tallies[1:1 + 2 * couples:2], tallies[2:2 + 2 * couples:2]
    slack = jnp.minimum(source_of - 1, reach - receiver)
    passed = jax.random.randint(jax.random.fold_in(stream_key, 1), (couples,), 0, 1 << 20) % (slack + 1)
    tallies = tallies.at[1:1 + 2 * couples:2].set(source_of - passed).at[2:2 + 2 * couples:2].set(receiver + passed)
    return tallies[jax.random.permutation(jax.random.fold_in(stream_key, 2), number_of)]


def scatter_about(stream_key, shape, spread, limit, pieces=(), kind=jnp.bfloat16):
    result = jax.random.normal(stream_key, shape, jnp.float32) * spread
    if len(pieces) > 0:
        result = block_levels(stream_key, shape, pieces, -0.22, 0.18) * result
    return jnp.clip(result, min=-limit, max=limit).astype(kind)


def setup_inputs(seed: int = 0, part: int = 0) -> dict:
    key_list = jax.random.split(jax.random.key(seed), 6)
    part_keys = jax.random.split(jax.random.fold_in(key_list[5], part), 6)
    queries = draw_queries(jax.random.fold_in(jax.random.fold_in(key_list[5], part), 71), part)
    key_states = draw_key_states(jax.random.fold_in(jax.random.fold_in(key_list[5], part), 71), part)
    value_states = scatter_about(part_keys[2], (TOKENS, HD), 1.0, 6.0, ((0, 8),))
    out_grad = scatter_about(part_keys[3], (TOKENS, H * HD), 1.0, 6.0, ((0, 8),))
    doc_ids = jnp.searchsorted(jnp.cumsum(ragged_sizes(part_keys[4], DOCS, TOKENS, MOST, 2)), jnp.arange(TOKENS), side="right").astype(jnp.int32)
    return dict(queries=queries, key_states=key_states, value_states=value_states, out_grad=out_grad, doc_ids=doc_ids)


def window_terms(query_rows, grad_rows, key_win, value_win, query_doc, window_doc):
    row_count = query_rows.shape[0]
    window = key_win.shape[0]
    head_dim = key_win.shape[1]
    head_count = query_rows.shape[1] // head_dim
    offset = window - row_count
    scaling = 1.0 / math.sqrt(head_dim)
    column = lax.broadcasted_iota(jnp.int32, (row_count, window), 1)
    row_index = lax.broadcasted_iota(jnp.int32, (row_count, window), 0)
    allowed = (window_doc[None, :] == query_doc[:, None]) & (column <= row_index + offset)
    allowed = jnp.concatenate([allowed, allowed], axis=0)

    def regroup(array):
        return array.reshape(row_count, head_count, head_dim).transpose(1, 0, 2).reshape(head_count // 2, 2 * row_count, head_dim)

    def one_group(totals, pair_rows):
        key_acc, value_acc = totals
        query_blk, grad_blk = pair_rows
        scores = scaling * jnp.dot(query_blk, key_win.T, preferred_element_type=jnp.float32)
        scores = jnp.where(allowed, scores, -1e+30)
        row_max = lax.optimization_barrier(jnp.max(scores, axis=1, keepdims=True))
        row_sum = lax.optimization_barrier(jnp.sum(jnp.exp(scores - row_max), axis=1, keepdims=True))
        weights = jnp.exp(scores - (row_max + jnp.log(row_sum)))
        prob_bf = weights.astype(jnp.bfloat16)
        out_rows = jnp.dot(prob_bf, value_win, preferred_element_type=jnp.float32).astype(jnp.bfloat16)
        row_dot = lax.optimization_barrier(jnp.sum(grad_blk.astype(jnp.float32) * out_rows.astype(jnp.float32), axis=1, keepdims=True))
        dprobs = jnp.dot(grad_blk, value_win.T, preferred_element_type=jnp.float32)
        dscores = (weights * (dprobs - row_dot)).astype(jnp.bfloat16)
        query_part = (scaling * jnp.dot(dscores, key_win, preferred_element_type=jnp.float32)).astype(jnp.bfloat16)
        key_acc = key_acc + scaling * jnp.dot(dscores.T, query_blk, preferred_element_type=jnp.float32)
        value_acc = value_acc + jnp.dot(prob_bf.T, grad_blk, preferred_element_type=jnp.float32)
        return ((key_acc, value_acc), (out_rows, query_part))
    zeroed = jnp.zeros((window, head_dim), jnp.float32)
    (key_acc, value_acc), (out_all, query_all) = lax.scan(one_group, (zeroed, zeroed), (regroup(query_rows), regroup(grad_rows)))

    def restore(array):
        return array.reshape(head_count, row_count, head_dim).transpose(1, 0, 2).reshape(row_count, head_count * head_dim)
    return (restore(out_all), restore(query_all), key_acc, value_acc)

def pair_order(array):
    blocks = array.reshape(2 * N_CTX, STRETCH, array.shape[1])
    lower_blocks = blocks[:N_CTX]
    upper_blocks = blocks[N_CTX:][::-1]
    return jnp.stack([lower_blocks, upper_blocks], axis=1).reshape(array.shape)

def reference(queries, key_states, value_states, out_grad, doc_ids):
    row_count = STRETCH
    padding = SPAN * STRETCH
    window_len = padding + row_count
    doc_all = doc_ids.astype(jnp.int32)
    key_padded = jnp.concatenate([jnp.zeros((padding, HD), key_states.dtype), key_states], axis=0)
    value_padded = jnp.concatenate([jnp.zeros((padding, HD), value_states.dtype), value_states], axis=0)
    doc_padded = jnp.concatenate([jnp.full((padding,), -1, jnp.int32), doc_all], axis=0)

    def one_block(totals, block_number):
        key_full, value_full = totals
        anchor = (block_number * row_count).astype(jnp.int32)
        query_rows = lax.dynamic_slice_in_dim(queries, anchor, row_count, 0)
        grad_rows = lax.dynamic_slice_in_dim(out_grad, anchor, row_count, 0)
        key_win = lax.dynamic_slice_in_dim(key_padded, anchor, window_len, 0)
        value_win = lax.dynamic_slice_in_dim(value_padded, anchor, window_len, 0)
        window_doc = lax.dynamic_slice_in_dim(doc_padded, anchor, window_len, 0)
        query_doc = lax.dynamic_slice_in_dim(doc_all, anchor, row_count, 0)
        out_rows, query_part, key_acc, value_acc = window_terms(query_rows, grad_rows, key_win, value_win, query_doc, window_doc)
        key_full = lax.dynamic_update_slice_in_dim(key_full, lax.dynamic_slice_in_dim(key_full, anchor, window_len, 0) + key_acc, anchor, 0)
        value_full = lax.dynamic_update_slice_in_dim(value_full, lax.dynamic_slice_in_dim(value_full, anchor, window_len, 0) + value_acc, anchor, 0)
        return ((key_full, value_full), (out_rows, query_part))
    zeroed = jnp.zeros((padding + TOKENS, HD), jnp.float32)
    (key_full, value_full), (out_all, query_all) = lax.scan(one_block, (zeroed, zeroed), jnp.arange(2 * N_CTX, dtype=jnp.int32))
    attn_seq = out_all.reshape(TOKENS, H * HD)
    query_seq = query_all.reshape(TOKENS, H * HD)
    return (pair_order(attn_seq), pair_order(query_seq), pair_order(key_full[padding:]), pair_order(value_full[padding:]))
```

```python
import functools
import math

import jax
import jax.numpy as jnp
from jax import lax
from jax.experimental import pallas as pl
from jax.experimental.pallas import tpu as pltpu
from jax.sharding import PartitionSpec as P

NEG_FILL = -1e30
LANES = 128
GROUP_HEADS = 2
MESH = pl.DeviceIdType.MESH


def kernel(
    members,
    halo,
    q_ref,
    k_ref,
    v_ref,
    g_ref,
    doc_ref,
    out_ref,
    dq_ref,
    dk_ref,
    dv_ref,
    window,
    out_stage,
    dq_stage,
    term_stage,
    term_in,
    kv_send,
    kv_recv,
    row_send,
    row_recv,
    term_send,
    term_recv,
):
    me = lax.axis_index("ctx")
    rows, width = q_ref.shape
    head_dim = k_ref.shape[1]
    heads = width // head_dim
    half_rows = rows // 2
    scaling = 1.0 / math.sqrt(head_dim)
    groups = heads // GROUP_HEADS
    keys = (halo + 1) * rows

    def place(block):
        upper = block >= members
        return jnp.where(upper, 2 * members - 1 - block, block), upper.astype(jnp.int32)

    def remote(src, dst, send, recv, target):
        return pltpu.make_async_remote_copy(
            src_ref=src,
            dst_ref=dst,
            send_sem=send,
            recv_sem=recv,
            device_id={"ctx": target},
            device_id_type=MESH,
        )

    sources = (me // 2, (2 * members - 1 - me) // 2)
    barrier = pltpu.get_barrier_semaphore()

    def greet(device):
        pl.semaphore_signal(barrier, inc=1, device_id={"ctx": device}, device_id_type=MESH)

    expected = jnp.int32(0)
    for j in range(1, halo + 1):
        pl.when(me - j >= 0)(functools.partial(greet, me - j))
        expected += (me + j < members).astype(jnp.int32)
    for j in range(halo + 1):
        for slot in range(2):
            source = sources[slot] + j
            pl.when((source < members) & (source != me))(functools.partial(greet, source))
        for half in range(2):
            target, _ = place(2 * (me - j) + half)
            expected += ((me - j >= 0) & (target != me)).astype(jnp.int32)
    pl.semaphore_wait(barrier, expected)

    def kv_copies(j, target):
        return [
            remote(ref, window.at[j - 1, i], kv_send.at[j - 1, i], kv_recv.at[j - 1, i], target)
            for i, ref in enumerate((k_ref, v_ref))
        ]

    for j in range(1, halo + 1):

        @pl.when(me + j < members)
        def _():
            for copy in kv_copies(j, me + j):
                copy.start()

    per_chunk = rows // LANES
    query_doc = jnp.concatenate(
        [doc_ref[pl.ds(me * per_chunk + i, 1), :] for i in range(per_chunk)], axis=1
    )
    columns = []
    for j in range(halo, -1, -1):
        chunk = me - j
        safe = jnp.maximum(chunk, 0)
        for i in range(per_chunk):
            row = doc_ref[pl.ds(safe * per_chunk + i, 1), :]
            column = jnp.broadcast_to(row, (LANES, LANES)).T
            columns.append(jnp.where(chunk >= 0, column, -1))
    key_doc = jnp.concatenate(columns, axis=0)
    key_doc = jnp.concatenate([key_doc] * per_chunk, axis=1)
    key_pos = lax.broadcasted_iota(jnp.int32, (keys, rows), 0) - halo * rows
    query_pos = lax.broadcasted_iota(jnp.int32, (keys, rows), 1)
    allowed = (key_doc == query_doc) & (key_pos <= query_pos)
    bias = jnp.where(allowed, 0.0, NEG_FILL)

    for j in range(1, halo + 1):

        @pl.when(me - j >= 0)
        def _():
            for copy in kv_copies(j, me):
                copy.wait_recv()

        @pl.when(me - j < 0)
        def _():
            window[j - 1] = jnp.zeros(window.shape[1:], window.dtype)

    key_win = jnp.concatenate([window[j - 1, 0] for j in range(halo, 0, -1)] + [k_ref[...]], axis=0)
    value_win = jnp.concatenate(
        [window[j - 1, 1] for j in range(halo, 0, -1)] + [v_ref[...]], axis=0
    )

    def dot(a, b, contract):
        return lax.dot_general(
            a, b, (((contract[0],), (contract[1],)), ((), ())), preferred_element_type=jnp.float32
        )

    def head(h, totals):
        key_acc, value_acc = totals
        at = pl.ds(pl.multiple_of(h * head_dim, head_dim), head_dim)
        q_head = q_ref[:, at]
        g_head = g_ref[:, at]
        scores = dot(key_win, q_head, (1, 1)) + bias
        top = jnp.max(scores, axis=0, keepdims=True)
        raised = jnp.exp2((scores - top) * (scaling * math.log2(math.e)))
        weights = raised * (1.0 / jnp.sum(raised, axis=0, keepdims=True))
        probs = weights.astype(jnp.bfloat16)
        dprobs = dot(value_win, g_head, (1, 1))
        row_dot = jnp.sum(weights * dprobs, axis=0, keepdims=True)
        dscores = (weights * (dprobs - row_dot)).astype(jnp.bfloat16)
        out_stage[:, at] = dot(probs, value_win, (0, 0)).astype(jnp.bfloat16)
        dq_stage[:, at] = (scaling * dot(dscores, key_win, (0, 0))).astype(jnp.bfloat16)
        return (key_acc + dot(dscores, q_head, (1, 0)), value_acc + dot(probs, g_head, (1, 0)))

    def row_copies(group, half, finish):
        target, slot = place(2 * me + half)
        at = pl.ds(group * GROUP_HEADS * head_dim, GROUP_HEADS * head_dim)
        here = pl.ds(half * half_rows, half_rows)
        there = pl.ds(pl.multiple_of(slot * half_rows, half_rows), half_rows)
        for i, (stage, result) in enumerate(((out_stage, out_ref), (dq_stage, dq_ref))):
            src, dst = stage.at[here, at], result.at[there, at]
            send, recv = row_send.at[group, half, i], row_recv.at[group, slot, i]
            yield src, dst, send, recv, target

    def term_copy(j, half):
        target, slot = place(2 * (me - j) + half)
        return (
            term_stage.at[j, half],
            term_in.at[slot, j],
            term_send.at[j, half],
            term_recv.at[slot, j],
            target,
        )

    def start(src, dst, send, recv, target):
        @pl.when(target != me)
        def _():
            remote(src, dst, send, recv, target).start()

        @pl.when(target == me)
        def _():
            pltpu.make_async_copy(src, dst, recv).start()

    def finish_send(src, dst, send, recv, target):
        @pl.when(target != me)
        def _():
            remote(src, dst, send, recv, target).wait_send()

    totals = (jnp.zeros((keys, head_dim), jnp.float32),) * 2
    for group in range(groups):
        first = group * GROUP_HEADS
        if rows * keys <= 256 * 256:
            for h in range(first, first + GROUP_HEADS):
                totals = head(h, totals)
        else:
            totals = lax.fori_loop(first, first + GROUP_HEADS, head, totals)
        for half in range(2):
            for copy in row_copies(group, half, False):
                start(*copy)

    for i, total in enumerate((totals[0] * scaling, totals[1])):
        total = total.astype(jnp.bfloat16)
        for j in range(halo + 1):
            for half in range(2):
                low = (halo - j) * rows + half * half_rows
                term_stage[j, half, i] = total[low : low + half_rows]
    for j in range(halo, -1, -1):

        @pl.when(me - j >= 0)
        def _():
            for half in range(2):
                start(*term_copy(j, half))

    for group in range(groups):
        at = pl.ds(group * GROUP_HEADS * head_dim, GROUP_HEADS * head_dim)
        for slot in range(2):
            there = pl.ds(slot * half_rows, half_rows)
            for i, (stage, result) in enumerate(((out_stage, out_ref), (dq_stage, dq_ref))):
                pltpu.make_async_copy(
                    stage.at[there, at], result.at[there, at], row_recv.at[group, slot, i]
                ).wait()
    for slot in range(2):
        for j in range(halo + 1):

            @pl.when(sources[slot] + j < members)
            def _():
                pltpu.make_async_copy(
                    term_stage.at[j, slot], term_in.at[slot, j], term_recv.at[slot, j]
                ).wait()

            @pl.when(sources[slot] + j >= members)
            def _():
                term_in[slot, j] = jnp.zeros(term_in.shape[2:], term_in.dtype)

        there = pl.ds(slot * half_rows, half_rows)
        for i, result in enumerate((dk_ref, dv_ref)):
            total = term_in[slot, 0, i].astype(jnp.float32)
            for j in range(1, halo + 1):
                total += term_in[slot, j, i].astype(jnp.float32)
            result[there, :] = total

    for j in range(1, halo + 1):

        @pl.when(me + j < members)
        def _():
            for copy in kv_copies(j, me + j):
                copy.wait_send()

    for group in range(groups):
        for half in range(2):
            for copy in row_copies(group, half, True):
                finish_send(*copy)
    for j in range(halo + 1):

        @pl.when(me - j >= 0)
        def _():
            for half in range(2):
                finish_send(*term_copy(j, half))


def shards(queries, key_states, value_states, out_grad, doc_ids):
    members = lax.axis_size("ctx")
    rows, width = queries.shape
    head_dim = key_states.shape[1]
    half_rows = rows // 2
    halo = -(-(members // 4) * half_rows // rows)
    groups = width // head_dim // GROUP_HEADS
    docs = doc_ids.reshape(doc_ids.shape[0] // LANES, LANES)
    vmem = pl.BlockSpec(memory_space=pltpu.VMEM)
    hbm = pl.BlockSpec(memory_space=pl.ANY)
    dma = pltpu.SemaphoreType.DMA
    keys = (halo + 1) * rows
    return pl.pallas_call(
        functools.partial(kernel, members, halo),
        out_shape=(
            jax.ShapeDtypeStruct((rows, width), jnp.bfloat16),
            jax.ShapeDtypeStruct((rows, width), jnp.bfloat16),
            jax.ShapeDtypeStruct((rows, head_dim), jnp.float32),
            jax.ShapeDtypeStruct((rows, head_dim), jnp.float32),
        ),
        in_specs=[vmem] * 5,
        out_specs=(hbm, hbm, vmem, vmem),
        scratch_shapes=[
            pltpu.VMEM((halo, 2, rows, head_dim), jnp.bfloat16),
            pltpu.VMEM((rows, width), jnp.bfloat16),
            pltpu.VMEM((rows, width), jnp.bfloat16),
            pltpu.VMEM((halo + 1, 2, 2, half_rows, head_dim), jnp.bfloat16),
            pltpu.VMEM((2, halo + 1, 2, half_rows, head_dim), jnp.bfloat16),
            dma((halo, 2)),
            dma((halo, 2)),
            dma((groups, 2, 2)),
            dma((groups, 2, 2)),
            dma((halo + 1, 2)),
            dma((2, halo + 1)),
        ],
        compiler_params=pltpu.CompilerParams(
            collective_id=0, has_side_effects=True, vmem_limit_bytes=40 * 1024 * 1024
        ),
        cost_estimate=pl.CostEstimate(
            flops=12 * rows * keys * width,
            bytes_accessed=8 * rows * width + 12 * rows * head_dim,
            transcendentals=rows * keys * width // head_dim,
        ),
    )(queries, key_states, value_states, out_grad, docs)


def solution(mesh):
    placed = P(("grp", "ctx"), None)
    return jax.shard_map(
        shards,
        mesh=mesh,
        in_specs=(placed, placed, placed, placed, P("grp")),
        out_specs=(placed,) * 4,
        check_vma=False,
    )
```

```python
import functools
import math

import jax
import jax.numpy as jnp
from jax import lax
from jax.experimental import pallas as pl
from jax.experimental.pallas import tpu as pltpu
from jax.sharding import PartitionSpec as P

NEG_FILL = -1e30
LANES = 128
GROUP_HEADS = 2
MESH = pl.DeviceIdType.MESH


def kernel(
    members,
    halo,
    q_hbm,
    k_hbm,
    v_hbm,
    g_hbm,
    doc_hbm,
    out_ref,
    dq_ref,
    term_in,
    q_ref,
    k_ref,
    v_ref,
    g_ref,
    doc_ref,
    window,
    out_stage,
    dq_stage,
    term_stage,
    load_sem,
    kv_send,
    kv_recv,
    row_send,
    row_recv,
    term_send,
    term_recv,
):
    me = lax.axis_index("ctx")
    rows, width = q_ref.shape
    head_dim = k_ref.shape[1]
    heads = width // head_dim
    half_rows = rows // 2
    scaling = 1.0 / math.sqrt(head_dim)
    groups = heads // GROUP_HEADS
    keys = (halo + 1) * rows

    loads = [
        pltpu.make_async_copy(src, dst, load_sem.at[i])
        for i, (src, dst) in enumerate(
            (
                (doc_hbm, doc_ref),
                (k_hbm, k_ref),
                (v_hbm, v_ref),
                (q_hbm, q_ref),
                (g_hbm, g_ref),
            )
        )
    ]
    for load in loads:
        load.start()

    def place(block):
        upper = block >= members
        return jnp.where(upper, 2 * members - 1 - block, block), upper.astype(jnp.int32)

    def remote(src, dst, send, recv, target):
        return pltpu.make_async_remote_copy(
            src_ref=src,
            dst_ref=dst,
            send_sem=send,
            recv_sem=recv,
            device_id={"ctx": target},
            device_id_type=MESH,
        )

    sources = (me // 2, (2 * members - 1 - me) // 2)
    barrier = pltpu.get_barrier_semaphore()

    def greet(device):
        pl.semaphore_signal(barrier, inc=1, device_id={"ctx": device}, device_id_type=MESH)

    expected = jnp.int32(0)
    for j in range(1, halo + 1):
        pl.when(me - j >= 0)(functools.partial(greet, me - j))
        expected += (me + j < members).astype(jnp.int32)
    for j in range(halo + 1):
        for slot in range(2):
            source = sources[slot] + j
            pl.when((source < members) & (source != me))(functools.partial(greet, source))
        for half in range(2):
            target, _ = place(2 * (me - j) + half)
            expected += ((me - j >= 0) & (target != me)).astype(jnp.int32)
    pl.semaphore_wait(barrier, expected)

    def kv_copies(j, target):
        return [
            remote(ref, window.at[j - 1, i], kv_send.at[j - 1, i], kv_recv.at[j - 1, i], target)
            for i, ref in enumerate((k_hbm, v_hbm))
        ]

    for j in range(1, halo + 1):

        @pl.when(me + j < members)
        def _():
            for copy in kv_copies(j, me + j):
                copy.start()

    loads[0].wait()

    per_chunk = rows // LANES
    query_doc = jnp.concatenate(
        [doc_ref[pl.ds(me * per_chunk + i, 1), :] for i in range(per_chunk)], axis=1
    )
    columns = []
    for j in range(halo, -1, -1):
        chunk = me - j
        safe = jnp.maximum(chunk, 0)
        for i in range(per_chunk):
            row = doc_ref[pl.ds(safe * per_chunk + i, 1), :]
            column = jnp.broadcast_to(row, (LANES, LANES)).T
            columns.append(jnp.where(chunk >= 0, column, -1))
    key_doc = jnp.concatenate(columns, axis=0)
    key_doc = jnp.concatenate([key_doc] * per_chunk, axis=1)
    key_pos = lax.broadcasted_iota(jnp.int32, (keys, rows), 0) - halo * rows
    query_pos = lax.broadcasted_iota(jnp.int32, (keys, rows), 1)
    allowed = (key_doc == query_doc) & (key_pos <= query_pos)
    bias = jnp.where(allowed, 0.0, NEG_FILL)

    for load in loads[1:]:
        load.wait()
    for j in range(1, halo + 1):

        @pl.when(me - j >= 0)
        def _():
            for copy in kv_copies(j, me):
                copy.wait_recv()

        @pl.when(me - j < 0)
        def _():
            window[j - 1] = jnp.zeros(window.shape[1:], window.dtype)

    key_win = jnp.concatenate([window[j - 1, 0] for j in range(halo, 0, -1)] + [k_ref[...]], axis=0)
    value_win = jnp.concatenate(
        [window[j - 1, 1] for j in range(halo, 0, -1)] + [v_ref[...]], axis=0
    )

    def dot(a, b, contract):
        return lax.dot_general(
            a, b, (((contract[0],), (contract[1],)), ((), ())), preferred_element_type=jnp.float32
        )

    def head(h, totals):
        key_acc, value_acc = totals
        at = pl.ds(pl.multiple_of(h * head_dim, head_dim), head_dim)
        q_head = q_ref[:, at]
        g_head = g_ref[:, at]
        scores = dot(key_win, q_head, (1, 1)) + bias
        top = jnp.max(scores, axis=0, keepdims=True)
        raised = jnp.exp2((scores - top) * (scaling * math.log2(math.e)))
        weights = raised * (1.0 / jnp.sum(raised, axis=0, keepdims=True))
        probs = weights.astype(jnp.bfloat16)
        dprobs = dot(value_win, g_head, (1, 1))
        row_dot = jnp.sum(weights * dprobs, axis=0, keepdims=True)
        dscores = (weights * (dprobs - row_dot)).astype(jnp.bfloat16)
        out_stage[:, at] = dot(probs, value_win, (0, 0)).astype(jnp.bfloat16)
        dq_stage[:, at] = (scaling * dot(dscores, key_win, (0, 0))).astype(jnp.bfloat16)
        return (key_acc + dot(dscores, q_head, (1, 0)), value_acc + dot(probs, g_head, (1, 0)))

    def row_copies(group, half, finish):
        target, slot = place(2 * me + half)
        at = pl.ds(group * GROUP_HEADS * head_dim, GROUP_HEADS * head_dim)
        here = pl.ds(half * half_rows, half_rows)
        there = pl.ds(pl.multiple_of(slot * half_rows, half_rows), half_rows)
        for i, (stage, result) in enumerate(((out_stage, out_ref), (dq_stage, dq_ref))):
            src, dst = stage.at[here, at], result.at[there, at]
            send, recv = row_send.at[group, half, i], row_recv.at[group, slot, i]
            yield src, dst, send, recv, target

    def term_copy(j, half):
        target, slot = place(2 * (me - j) + half)
        return (
            term_stage.at[j, half],
            term_in.at[slot, j],
            term_send.at[j, half],
            term_recv.at[slot, j],
            target,
        )

    def start(src, dst, send, recv, target):
        @pl.when(target != me)
        def _():
            remote(src, dst, send, recv, target).start()

        @pl.when(target == me)
        def _():
            pltpu.make_async_copy(src, dst, recv).start()

    def finish_send(src, dst, send, recv, target):
        @pl.when(target != me)
        def _():
            remote(src, dst, send, recv, target).wait_send()

    totals = (jnp.zeros((keys, head_dim), jnp.float32),) * 2
    for group in range(groups):
        first = group * GROUP_HEADS
        if rows * keys <= 256 * 256:
            for h in range(first, first + GROUP_HEADS):
                totals = head(h, totals)
        else:
            totals = lax.fori_loop(first, first + GROUP_HEADS, head, totals)
        for half in range(2):
            for copy in row_copies(group, half, False):
                start(*copy)

    for i, total in enumerate((totals[0] * scaling, totals[1])):
        total = total.astype(jnp.bfloat16)
        for j in range(halo + 1):
            for half in range(2):
                low = (halo - j) * rows + half * half_rows
                term_stage[j, half, i] = total[low : low + half_rows]
    for j in range(halo, -1, -1):

        @pl.when(me - j >= 0)
        def _():
            for half in range(2):
                start(*term_copy(j, half))

    for group in range(groups):
        at = pl.ds(group * GROUP_HEADS * head_dim, GROUP_HEADS * head_dim)
        for slot in range(2):
            there = pl.ds(slot * half_rows, half_rows)
            for i, (stage, result) in enumerate(((out_stage, out_ref), (dq_stage, dq_ref))):
                pltpu.make_async_copy(
                    stage.at[there, at], result.at[there, at], row_recv.at[group, slot, i]
                ).wait()
    for slot in range(2):
        for j in range(halo + 1):

            @pl.when(sources[slot] + j < members)
            def _():
                pltpu.make_async_copy(
                    term_stage.at[j, slot], term_in.at[slot, j], term_recv.at[slot, j]
                ).wait()

            @pl.when(sources[slot] + j >= members)
            def _():
                term_in[slot, j] = jnp.zeros(term_in.shape[2:], term_in.dtype)

    for j in range(1, halo + 1):

        @pl.when(me + j < members)
        def _():
            for copy in kv_copies(j, me + j):
                copy.wait_send()

    for group in range(groups):
        for half in range(2):
            for copy in row_copies(group, half, True):
                finish_send(*copy)
    for j in range(halo + 1):

        @pl.when(me - j >= 0)
        def _():
            for half in range(2):
                finish_send(*term_copy(j, half))


def finish(out_in, dq_in, terms, out_ref, dq_ref, dk_ref, dv_ref, grads, sems):
    rows = [
        pltpu.make_async_copy(out_in, out_ref, sems.at[0]),
        pltpu.make_async_copy(dq_in, dq_ref, sems.at[1]),
    ]
    for copy in rows:
        copy.start()
    half_rows = terms.shape[3]
    for i, result in enumerate((dk_ref, dv_ref)):
        for slot in range(2):
            total = terms[slot, 0, i].astype(jnp.float32)
            for j in range(1, terms.shape[1]):
                total += terms[slot, j, i].astype(jnp.float32)
            grads[i, pl.ds(slot * half_rows, half_rows), :] = total
        copy = pltpu.make_async_copy(grads.at[i], result, sems.at[2 + i])
        copy.start()
        rows.append(copy)
    for copy in rows:
        copy.wait()


def shards(queries, key_states, value_states, out_grad, doc_ids):
    members = lax.axis_size("ctx")
    rows, width = queries.shape
    head_dim = key_states.shape[1]
    half_rows = rows // 2
    halo = -(-(members // 4) * half_rows // rows)
    groups = width // head_dim // GROUP_HEADS
    docs = doc_ids.reshape(doc_ids.shape[0] // LANES, LANES)
    vmem = pl.BlockSpec(memory_space=pltpu.VMEM)
    hbm = pl.BlockSpec(memory_space=pltpu.HBM)
    anywhere = pl.BlockSpec(memory_space=pl.ANY)
    dma = pltpu.SemaphoreType.DMA
    keys = (halo + 1) * rows
    row_shape = jax.ShapeDtypeStruct((rows, width), jnp.bfloat16)
    grad_shape = jax.ShapeDtypeStruct((rows, head_dim), jnp.float32)
    operands = (queries, key_states, value_states, out_grad, docs)
    out_rows, dq_rows, terms = pl.pallas_call(
        functools.partial(kernel, members, halo),
        out_shape=(
            row_shape,
            row_shape,
            jax.ShapeDtypeStruct((2, halo + 1, 2, half_rows, head_dim), jnp.bfloat16),
        ),
        in_specs=[hbm] * 5,
        out_specs=(vmem, vmem, vmem),
        scratch_shapes=[
            pltpu.VMEM((rows, width), jnp.bfloat16),
            pltpu.VMEM((rows, head_dim), jnp.bfloat16),
            pltpu.VMEM((rows, head_dim), jnp.bfloat16),
            pltpu.VMEM((rows, width), jnp.bfloat16),
            pltpu.VMEM(docs.shape, jnp.int32),
            pltpu.VMEM((halo, 2, rows, head_dim), jnp.bfloat16),
            pltpu.VMEM((rows, width), jnp.bfloat16),
            pltpu.VMEM((rows, width), jnp.bfloat16),
            pltpu.VMEM((halo + 1, 2, 2, half_rows, head_dim), jnp.bfloat16),
            dma((5,)),
            dma((halo, 2)),
            dma((halo, 2)),
            dma((groups, 2, 2)),
            dma((groups, 2, 2)),
            dma((halo + 1, 2)),
            dma((2, halo + 1)),
        ],
        compiler_params=pltpu.CompilerParams(
            collective_id=0, has_side_effects=True, vmem_limit_bytes=40 * 1024 * 1024
        ),
        cost_estimate=pl.CostEstimate(
            flops=12 * rows * keys * width,
            bytes_accessed=8 * rows * width + 12 * rows * head_dim,
            transcendentals=rows * keys * width // head_dim,
        ),
    )(*(pltpu.with_memory_space_constraint(x, pltpu.HBM) for x in operands))
    return pl.pallas_call(
        finish,
        out_shape=(row_shape, row_shape, grad_shape, grad_shape),
        in_specs=[anywhere, anywhere, vmem],
        out_specs=(hbm,) * 4,
        scratch_shapes=[pltpu.VMEM((2, rows, head_dim), jnp.float32), dma((4,))],
        compiler_params=pltpu.CompilerParams(vmem_limit_bytes=16 * 1024 * 1024),
    )(out_rows, dq_rows, terms)


def solution(mesh):
    placed = P(("grp", "ctx"), None)
    return jax.shard_map(
        shards,
        mesh=mesh,
        in_specs=(placed, placed, placed, placed, P("grp")),
        out_specs=(placed,) * 4,
        check_vma=False,
    )
```

```python
import functools
import math

import jax
import jax.numpy as jnp
from jax import lax
from jax.experimental import pallas as pl
from jax.experimental.pallas import tpu as pltpu
from jax.sharding import PartitionSpec as P

NEG_FILL = -1e30
LANES = 128
GROUP_HEADS = 2
MESH = pl.DeviceIdType.MESH


def kernel(
    members,
    halo,
    q_hbm,
    k_hbm,
    v_hbm,
    g_hbm,
    doc_hbm,
    out_ref,
    dq_ref,
    term_in,
    q_ref,
    k_ref,
    v_ref,
    g_ref,
    doc_ref,
    window,
    out_stage,
    dq_stage,
    term_stage,
    weights,
    dprobs_own,
    load_sem,
    kv_send,
    kv_recv,
    row_send,
    row_recv,
    term_send,
    term_recv,
):
    me = lax.axis_index("ctx")
    rows, width = q_ref.shape
    head_dim = k_ref.shape[1]
    heads = width // head_dim
    half_rows = rows // 2
    scaling = 1.0 / math.sqrt(head_dim)
    groups = heads // GROUP_HEADS
    keys = (halo + 1) * rows

    loads = [
        pltpu.make_async_copy(src, dst, load_sem.at[i])
        for i, (src, dst) in enumerate(
            (
                (doc_hbm, doc_ref),
                (k_hbm, k_ref),
                (v_hbm, v_ref),
                (q_hbm, q_ref),
                (g_hbm, g_ref),
            )
        )
    ]
    for load in loads:
        load.start()

    def place(block):
        upper = block >= members
        return jnp.where(upper, 2 * members - 1 - block, block), upper.astype(jnp.int32)

    def remote(src, dst, send, recv, target):
        return pltpu.make_async_remote_copy(
            src_ref=src,
            dst_ref=dst,
            send_sem=send,
            recv_sem=recv,
            device_id={"ctx": target},
            device_id_type=MESH,
        )

    sources = (me // 2, (2 * members - 1 - me) // 2)
    barrier = pltpu.get_barrier_semaphore()

    def greet(device):
        pl.semaphore_signal(barrier, inc=1, device_id={"ctx": device}, device_id_type=MESH)

    expected = jnp.int32(0)
    for j in range(1, halo + 1):
        pl.when(me - j >= 0)(functools.partial(greet, me - j))
        expected += (me + j < members).astype(jnp.int32)
    for j in range(halo + 1):
        for slot in range(2):
            source = sources[slot] + j
            pl.when((source < members) & (source != me))(functools.partial(greet, source))
        for half in range(2):
            target, _ = place(2 * (me - j) + half)
            expected += ((me - j >= 0) & (target != me)).astype(jnp.int32)
    pl.semaphore_wait(barrier, expected)

    def kv_copies(j, target):
        return [
            remote(ref, window.at[j - 1, i], kv_send.at[j - 1, i], kv_recv.at[j - 1, i], target)
            for i, ref in enumerate((k_hbm, v_hbm))
        ]

    for j in range(1, halo + 1):

        @pl.when(me + j < members)
        def _():
            for copy in kv_copies(j, me + j):
                copy.start()

    loads[0].wait()

    per_chunk = rows // LANES
    query_doc = jnp.concatenate(
        [doc_ref[pl.ds(me * per_chunk + i, 1), :] for i in range(per_chunk)], axis=1
    )
    columns = []
    for j in range(halo, -1, -1):
        chunk = me - j
        safe = jnp.maximum(chunk, 0)
        for i in range(per_chunk):
            row = doc_ref[pl.ds(safe * per_chunk + i, 1), :]
            column = jnp.broadcast_to(row, (LANES, LANES)).T
            columns.append(jnp.where(chunk >= 0, column, -1))
    key_doc = jnp.concatenate(columns, axis=0)
    key_doc = jnp.concatenate([key_doc] * per_chunk, axis=1)
    key_pos = lax.broadcasted_iota(jnp.int32, (keys, rows), 0) - halo * rows
    query_pos = lax.broadcasted_iota(jnp.int32, (keys, rows), 1)
    allowed = (key_doc == query_doc) & (key_pos <= query_pos)
    bias = jnp.where(allowed, 0.0, NEG_FILL)

    for load in loads[1:]:
        load.wait()

    def dot(a, b, contract):
        return lax.dot_general(
            a, b, (((contract[0],), (contract[1],)), ((), ())), preferred_element_type=jnp.float32
        )

    def columns_of(h):
        return pl.ds(pl.multiple_of(h * head_dim, head_dim), head_dim)

    def queries_of(h):
        return pl.ds(pl.multiple_of(h * rows, rows), rows)

    unrolled = rows * keys <= 256 * 256

    def each_head(first, last, body, state):
        if not unrolled:
            return lax.fori_loop(first, last, body, state)
        for h in range(first, last):
            state = body(h, state)
        return state

    below = halo * rows
    own = pl.ds(below, rows)
    earlier = pl.ds(0, below)

    def own_head(h, state):
        scores = dot(k_ref[...], q_ref[:, columns_of(h)], (1, 1))
        weights[own, queries_of(h)] = scores + bias[below:]
        dprobs_own[:, queries_of(h)] = dot(v_ref[...], g_ref[:, columns_of(h)], (1, 1))
        return state

    each_head(0, heads, own_head, 0)

    for j in range(1, halo + 1):

        @pl.when(me - j >= 0)
        def _():
            for copy in kv_copies(j, me):
                copy.wait_recv()

        @pl.when(me - j < 0)
        def _():
            window[j - 1] = jnp.zeros(window.shape[1:], window.dtype)

    key_low = jnp.concatenate([window[j - 1, 0] for j in range(halo, 0, -1)], axis=0)
    value_low = jnp.concatenate([window[j - 1, 1] for j in range(halo, 0, -1)], axis=0)
    key_win = jnp.concatenate([key_low, k_ref[...]], axis=0)
    value_win = jnp.concatenate([value_low, v_ref[...]], axis=0)

    def forward(group):
        def head(h, state):
            at = queries_of(h)
            low = dot(key_low, q_ref[:, columns_of(h)], (1, 1)) + bias[:below]
            scores = jnp.concatenate([low, weights[own, at]], axis=0)
            top = jnp.max(scores, axis=0, keepdims=True)
            raised = jnp.exp2((scores - top) * (scaling * math.log2(math.e)))
            weight = raised * (1.0 / jnp.sum(raised, axis=0, keepdims=True))
            weights[:, at] = weight
            out = dot(weight.astype(jnp.bfloat16), value_win, (0, 0))
            out_stage[group, :, columns_of(h - group * GROUP_HEADS)] = out.astype(jnp.bfloat16)
            return state

        return head

    def backward(group):
        def head(h, totals):
            key_acc, value_acc = totals
            at = queries_of(h)
            q_head = q_ref[:, columns_of(h)]
            g_head = g_ref[:, columns_of(h)]
            weight = weights[:, at]
            dprobs = jnp.concatenate([dot(value_low, g_head, (1, 1)), dprobs_own[:, at]], axis=0)
            row_dot = jnp.sum(weight * dprobs, axis=0, keepdims=True)
            dscores = (weight * (dprobs - row_dot)).astype(jnp.bfloat16)
            query_part = scaling * dot(dscores, key_win, (0, 0))
            dq_stage[group, :, columns_of(h - group * GROUP_HEADS)] = query_part.astype(jnp.bfloat16)
            return (
                key_acc + dot(dscores, q_head, (1, 0)),
                value_acc + dot(weight.astype(jnp.bfloat16), g_head, (1, 0)),
            )

        return head

    staged = ((out_stage, out_ref), (dq_stage, dq_ref))

    def row_copy(i, group, half):
        target, slot = place(2 * me + half)
        here = pl.ds(half * half_rows, half_rows)
        there = pl.ds(pl.multiple_of(slot * half_rows, half_rows), half_rows)
        return (
            staged[i][0].at[group, here],
            staged[i][1].at[group, there],
            row_send.at[group, half, i],
            row_recv.at[group, slot, i],
            target,
        )

    def term_copy(j, half):
        target, slot = place(2 * (me - j) + half)
        return (
            term_stage.at[j, half],
            term_in.at[slot, j],
            term_send.at[j, half],
            term_recv.at[slot, j],
            target,
        )

    def start(src, dst, send, recv, target):
        @pl.when(target != me)
        def _():
            remote(src, dst, send, recv, target).start()

        @pl.when(target == me)
        def _():
            pltpu.make_async_copy(src, dst, recv).start()

    def finish_send(src, dst, send, recv, target):
        @pl.when(target != me)
        def _():
            remote(src, dst, send, recv, target).wait_send()

    for group in range(groups):
        first = group * GROUP_HEADS
        each_head(first, first + GROUP_HEADS, forward(group), 0)
        for half in range(2):
            start(*row_copy(0, group, half))
    totals = (jnp.zeros((keys, head_dim), jnp.float32),) * 2
    for group in range(groups):
        first = group * GROUP_HEADS
        totals = each_head(first, first + GROUP_HEADS, backward(group), totals)
        for half in range(2):
            start(*row_copy(1, group, half))

    for i, total in enumerate((totals[0] * scaling, totals[1])):
        total = total.astype(jnp.bfloat16)
        for j in range(halo + 1):
            for half in range(2):
                low = (halo - j) * rows + half * half_rows
                term_stage[j, half, i] = total[low : low + half_rows]
    for j in range(halo, -1, -1):

        @pl.when(me - j >= 0)
        def _():
            for half in range(2):
                start(*term_copy(j, half))

    for i, (stage, result) in enumerate(staged):
        for group in range(groups):
            for slot in range(2):
                there = pl.ds(slot * half_rows, half_rows)
                pltpu.make_async_copy(
                    stage.at[group, there], result.at[group, there], row_recv.at[group, slot, i]
                ).wait()
    for slot in range(2):
        for j in range(halo + 1):

            @pl.when(sources[slot] + j < members)
            def _():
                pltpu.make_async_copy(
                    term_stage.at[j, slot], term_in.at[slot, j], term_recv.at[slot, j]
                ).wait()

            @pl.when(sources[slot] + j >= members)
            def _():
                term_in[slot, j] = jnp.zeros(term_in.shape[2:], term_in.dtype)

    for j in range(1, halo + 1):

        @pl.when(me + j < members)
        def _():
            for copy in kv_copies(j, me + j):
                copy.wait_send()

    for group in range(groups):
        for half in range(2):
            for i in range(2):
                finish_send(*row_copy(i, group, half))
    for j in range(halo + 1):

        @pl.when(me - j >= 0)
        def _():
            for half in range(2):
                finish_send(*term_copy(j, half))


def finish(out_in, dq_in, terms, out_ref, dq_ref, dk_ref, dv_ref, grads, row_sems, sems):
    groups, _, group_width = out_in.shape
    rows = []
    for group in range(groups):
        at = pl.ds(group * group_width, group_width)
        for i, (src, dst) in enumerate(((out_in, out_ref), (dq_in, dq_ref))):
            rows.append(
                pltpu.make_async_copy(src.at[group], dst.at[:, at], row_sems.at[i, group])
            )
    for copy in rows:
        copy.start()
    half_rows = terms.shape[3]
    for i, result in enumerate((dk_ref, dv_ref)):
        for slot in range(2):
            total = terms[slot, 0, i].astype(jnp.float32)
            for j in range(1, terms.shape[1]):
                total += terms[slot, j, i].astype(jnp.float32)
            grads[i, pl.ds(slot * half_rows, half_rows), :] = total
        copy = pltpu.make_async_copy(grads.at[i], result, sems.at[i])
        copy.start()
        rows.append(copy)
    for copy in rows:
        copy.wait()


def shards(queries, key_states, value_states, out_grad, doc_ids):
    members = lax.axis_size("ctx")
    rows, width = queries.shape
    head_dim = key_states.shape[1]
    half_rows = rows // 2
    halo = -(-(members // 4) * half_rows // rows)
    groups = width // head_dim // GROUP_HEADS
    docs = doc_ids.reshape(doc_ids.shape[0] // LANES, LANES)
    vmem = pl.BlockSpec(memory_space=pltpu.VMEM)
    hbm = pl.BlockSpec(memory_space=pltpu.HBM)
    anywhere = pl.BlockSpec(memory_space=pl.ANY)
    dma = pltpu.SemaphoreType.DMA
    keys = (halo + 1) * rows
    group_shape = jax.ShapeDtypeStruct((groups, rows, GROUP_HEADS * head_dim), jnp.bfloat16)
    row_shape = jax.ShapeDtypeStruct((rows, width), jnp.bfloat16)
    grad_shape = jax.ShapeDtypeStruct((rows, head_dim), jnp.float32)
    operands = (queries, key_states, value_states, out_grad, docs)
    out_rows, dq_rows, terms = pl.pallas_call(
        functools.partial(kernel, members, halo),
        out_shape=(
            group_shape,
            group_shape,
            jax.ShapeDtypeStruct((2, halo + 1, 2, half_rows, head_dim), jnp.bfloat16),
        ),
        in_specs=[hbm] * 5,
        out_specs=(vmem, vmem, vmem),
        scratch_shapes=[
            pltpu.VMEM((rows, width), jnp.bfloat16),
            pltpu.VMEM((rows, head_dim), jnp.bfloat16),
            pltpu.VMEM((rows, head_dim), jnp.bfloat16),
            pltpu.VMEM((rows, width), jnp.bfloat16),
            pltpu.VMEM(docs.shape, jnp.int32),
            pltpu.VMEM((halo, 2, rows, head_dim), jnp.bfloat16),
            pltpu.VMEM(group_shape.shape, jnp.bfloat16),
            pltpu.VMEM(group_shape.shape, jnp.bfloat16),
            pltpu.VMEM((halo + 1, 2, 2, half_rows, head_dim), jnp.bfloat16),
            pltpu.VMEM((keys, width // head_dim * rows), jnp.float32),
            pltpu.VMEM((rows, width // head_dim * rows), jnp.float32),
            dma((5,)),
            dma((halo, 2)),
            dma((halo, 2)),
            dma((groups, 2, 2)),
            dma((groups, 2, 2)),
            dma((halo + 1, 2)),
            dma((2, halo + 1)),
        ],
        compiler_params=pltpu.CompilerParams(
            collective_id=0, has_side_effects=True, vmem_limit_bytes=40 * 1024 * 1024
        ),
        cost_estimate=pl.CostEstimate(
            flops=12 * rows * keys * width,
            bytes_accessed=8 * rows * width + 12 * rows * head_dim,
            transcendentals=rows * keys * width // head_dim,
        ),
    )(*(pltpu.with_memory_space_constraint(x, pltpu.HBM) for x in operands))
    return pl.pallas_call(
        finish,
        out_shape=(row_shape, row_shape, grad_shape, grad_shape),
        in_specs=[anywhere, anywhere, vmem],
        out_specs=(hbm,) * 4,
        scratch_shapes=[pltpu.VMEM((2, rows, head_dim), jnp.float32), dma((2, groups)), dma((2,))],
        compiler_params=pltpu.CompilerParams(vmem_limit_bytes=16 * 1024 * 1024),
    )(out_rows, dq_rows, terms)


def solution(mesh):
    placed = P(("grp", "ctx"), None)
    return jax.shard_map(
        shards,
        mesh=mesh,
        in_specs=(placed, placed, placed, placed, P("grp")),
        out_specs=(placed,) * 4,
        check_vma=False,
    )
```

```python
import functools
import math

import jax
import jax.numpy as jnp
from jax import lax
from jax.experimental import pallas as pl
from jax.experimental.pallas import tpu as pltpu
from jax.sharding import PartitionSpec as P

NEG_FILL = -1e30
LANES = 128
GROUP_HEADS = 4
MESH = pl.DeviceIdType.MESH


def kernel(
    members,
    halo,
    q_hbm,
    k_hbm,
    v_hbm,
    g_hbm,
    doc_hbm,
    out_ref,
    dq_ref,
    term_in,
    q_ref,
    k_ref,
    v_ref,
    g_ref,
    doc_ref,
    window,
    out_stage,
    dq_stage,
    term_stage,
    weights,
    dprobs_own,
    load_sem,
    kv_send,
    kv_recv,
    row_send,
    row_recv,
    term_send,
    term_recv,
):
    me = lax.axis_index("ctx")
    rows, width = q_ref.shape
    head_dim = k_ref.shape[1]
    heads = width // head_dim
    half_rows = rows // 2
    scaling = 1.0 / math.sqrt(head_dim)
    groups = heads // GROUP_HEADS
    keys = (halo + 1) * rows

    loads = [
        pltpu.make_async_copy(src, dst, load_sem.at[i])
        for i, (src, dst) in enumerate(
            (
                (doc_hbm, doc_ref),
                (k_hbm, k_ref),
                (v_hbm, v_ref),
                (q_hbm, q_ref),
                (g_hbm, g_ref),
            )
        )
    ]
    def place(block):
        upper = block >= members
        return jnp.where(upper, 2 * members - 1 - block, block), upper.astype(jnp.int32)

    def remote(src, dst, send, recv, target):
        return pltpu.make_async_remote_copy(
            src_ref=src,
            dst_ref=dst,
            send_sem=send,
            recv_sem=recv,
            device_id={"ctx": target},
            device_id_type=MESH,
        )

    sources = (me // 2, (2 * members - 1 - me) // 2)
    barrier = pltpu.get_barrier_semaphore()

    def greet(device):
        pl.semaphore_signal(barrier, inc=1, device_id={"ctx": device}, device_id_type=MESH)

    expected = jnp.int32(0)
    for j in range(1, halo + 1):
        pl.when(me - j >= 0)(functools.partial(greet, me - j))
        expected += (me + j < members).astype(jnp.int32)
    for j in range(halo + 1):
        for slot in range(2):
            source = sources[slot] + j
            pl.when((source < members) & (source != me))(functools.partial(greet, source))
        for half in range(2):
            target, _ = place(2 * (me - j) + half)
            expected += ((me - j >= 0) & (target != me)).astype(jnp.int32)
    for load in loads:
        load.start()
    pl.semaphore_wait(barrier, expected)

    def kv_copies(j, target):
        return [
            remote(ref, window.at[j - 1, i], kv_send.at[j - 1, i], kv_recv.at[j - 1, i], target)
            for i, ref in enumerate((k_hbm, v_hbm))
        ]

    for j in range(1, halo + 1):

        @pl.when(me + j < members)
        def _():
            for copy in kv_copies(j, me + j):
                copy.start()

    loads[0].wait()

    per_chunk = rows // LANES
    query_doc = jnp.concatenate(
        [doc_ref[pl.ds(me * per_chunk + i, 1), :] for i in range(per_chunk)], axis=1
    )
    columns = []
    for j in range(halo, -1, -1):
        chunk = me - j
        safe = jnp.maximum(chunk, 0)
        for i in range(per_chunk):
            row = doc_ref[pl.ds(safe * per_chunk + i, 1), :]
            column = jnp.broadcast_to(row, (LANES, LANES)).T
            columns.append(jnp.where(chunk >= 0, column, -1))
    key_doc = jnp.concatenate(columns, axis=0)
    key_doc = jnp.concatenate([key_doc] * per_chunk, axis=1)
    key_pos = lax.broadcasted_iota(jnp.int32, (keys, rows), 0) - halo * rows
    query_pos = lax.broadcasted_iota(jnp.int32, (keys, rows), 1)
    allowed = (key_doc == query_doc) & (key_pos <= query_pos)
    bias = jnp.where(allowed, 0.0, NEG_FILL)

    for load in loads[1:]:
        load.wait()

    def dot(a, b, contract):
        return lax.dot_general(
            a, b, (((contract[0],), (contract[1],)), ((), ())), preferred_element_type=jnp.float32
        )

    def columns_of(h):
        return pl.ds(pl.multiple_of(h * head_dim, head_dim), head_dim)

    def queries_of(h):
        return pl.ds(pl.multiple_of(h * rows, rows), rows)

    unrolled = rows * keys <= 256 * 256

    def each_head(first, last, body, state):
        if not unrolled:
            return lax.fori_loop(first, last, body, state)
        for h in range(first, last):
            state = body(h, state)
        return state

    below = halo * rows
    own = pl.ds(below, rows)
    earlier = pl.ds(0, below)

    def own_head(h, state):
        scores = dot(k_ref[...], q_ref[:, columns_of(h)], (1, 1))
        weights[own, queries_of(h)] = scores + bias[below:]
        dprobs_own[:, queries_of(h)] = dot(v_ref[...], g_ref[:, columns_of(h)], (1, 1))
        return state

    each_head(0, heads, own_head, 0)

    for j in range(1, halo + 1):

        @pl.when(me - j >= 0)
        def _():
            for copy in kv_copies(j, me):
                copy.wait_recv()

        @pl.when(me - j < 0)
        def _():
            window[j - 1] = jnp.zeros(window.shape[1:], window.dtype)

    key_low = jnp.concatenate([window[j - 1, 0] for j in range(halo, 0, -1)], axis=0)
    value_low = jnp.concatenate([window[j - 1, 1] for j in range(halo, 0, -1)], axis=0)
    key_win = jnp.concatenate([key_low, k_ref[...]], axis=0)
    value_win = jnp.concatenate([value_low, v_ref[...]], axis=0)

    def forward(group):
        def head(h, state):
            at = queries_of(h)
            low = dot(key_low, q_ref[:, columns_of(h)], (1, 1)) + bias[:below]
            scores = jnp.concatenate([low, weights[own, at]], axis=0)
            top = jnp.max(scores, axis=0, keepdims=True)
            raised = jnp.exp2((scores - top) * (scaling * math.log2(math.e)))
            weight = raised * (1.0 / jnp.sum(raised, axis=0, keepdims=True))
            weights[:, at] = weight
            out = dot(weight.astype(jnp.bfloat16), value_win, (0, 0))
            out_stage[group, :, columns_of(h - group * GROUP_HEADS)] = out.astype(jnp.bfloat16)
            return state

        return head

    def backward(group):
        def head(h, totals):
            key_acc, value_acc = totals
            at = queries_of(h)
            q_head = q_ref[:, columns_of(h)]
            g_head = g_ref[:, columns_of(h)]
            weight = weights[:, at]
            dprobs = jnp.concatenate([dot(value_low, g_head, (1, 1)), dprobs_own[:, at]], axis=0)
            row_dot = jnp.sum(weight * dprobs, axis=0, keepdims=True)
            dscores = (weight * (dprobs - row_dot)).astype(jnp.bfloat16)
            query_part = scaling * dot(dscores, key_win, (0, 0))
            dq_stage[group, :, columns_of(h - group * GROUP_HEADS)] = query_part.astype(jnp.bfloat16)
            return (
                key_acc + dot(dscores, q_head, (1, 0)),
                value_acc + dot(weight.astype(jnp.bfloat16), g_head, (1, 0)),
            )

        return head

    staged = ((out_stage, out_ref), (dq_stage, dq_ref))

    def row_copy(i, group, half):
        target, slot = place(2 * me + half)
        here = pl.ds(half * half_rows, half_rows)
        there = pl.ds(pl.multiple_of(slot * half_rows, half_rows), half_rows)
        return (
            staged[i][0].at[group, here],
            staged[i][1].at[group, there],
            row_send.at[group, half, i],
            row_recv.at[group, slot, i],
            target,
        )

    def term_copy(j, half):
        target, slot = place(2 * (me - j) + half)
        return (
            term_stage.at[j, half],
            term_in.at[slot, j],
            term_send.at[j, half],
            term_recv.at[slot, j],
            target,
        )

    def start(src, dst, send, recv, target):
        @pl.when(target != me)
        def _():
            remote(src, dst, send, recv, target).start()

        @pl.when(target == me)
        def _():
            pltpu.make_async_copy(src, dst, recv).start()

    def finish_send(src, dst, send, recv, target):
        @pl.when(target != me)
        def _():
            remote(src, dst, send, recv, target).wait_send()

    for group in range(groups):
        first = group * GROUP_HEADS
        each_head(first, first + GROUP_HEADS, forward(group), 0)
        for half in range(2):
            start(*row_copy(0, group, half))
    totals = (jnp.zeros((keys, head_dim), jnp.float32),) * 2
    for group in range(groups):
        first = group * GROUP_HEADS
        totals = each_head(first, first + GROUP_HEADS, backward(group), totals)
        for half in range(2):
            start(*row_copy(1, group, half))

    for i, total in enumerate((totals[0] * scaling, totals[1])):
        total = total.astype(jnp.bfloat16)
        for j in range(halo + 1):
            for half in range(2):
                low = (halo - j) * rows + half * half_rows
                term_stage[j, half, i] = total[low : low + half_rows]
    for j in range(halo, -1, -1):

        @pl.when(me - j >= 0)
        def _():
            for half in range(2):
                start(*term_copy(j, half))

    for i, (stage, result) in enumerate(staged):
        for group in range(groups):
            for slot in range(2):
                there = pl.ds(slot * half_rows, half_rows)
                pltpu.make_async_copy(
                    stage.at[group, there], result.at[group, there], row_recv.at[group, slot, i]
                ).wait()
    for slot in range(2):
        for j in range(halo + 1):

            @pl.when(sources[slot] + j < members)
            def _():
                pltpu.make_async_copy(
                    term_stage.at[j, slot], term_in.at[slot, j], term_recv.at[slot, j]
                ).wait()

            @pl.when(sources[slot] + j >= members)
            def _():
                term_in[slot, j] = jnp.zeros(term_in.shape[2:], term_in.dtype)

    for j in range(1, halo + 1):

        @pl.when(me + j < members)
        def _():
            for copy in kv_copies(j, me + j):
                copy.wait_send()

    for group in range(groups):
        for half in range(2):
            for i in range(2):
                finish_send(*row_copy(i, group, half))
    for j in range(halo + 1):

        @pl.when(me - j >= 0)
        def _():
            for half in range(2):
                finish_send(*term_copy(j, half))


def finish(out_in, dq_in, terms, out_ref, dq_ref, dk_ref, dv_ref, grads, row_sems, sems):
    groups, _, group_width = out_in.shape
    rows = []
    for group in range(groups):
        at = pl.ds(group * group_width, group_width)
        for i, (src, dst) in enumerate(((out_in, out_ref), (dq_in, dq_ref))):
            rows.append(
                pltpu.make_async_copy(src.at[group], dst.at[:, at], row_sems.at[i, group])
            )
    for copy in rows:
        copy.start()
    half_rows = terms.shape[3]
    for i, result in enumerate((dk_ref, dv_ref)):
        for slot in range(2):
            total = terms[slot, 0, i].astype(jnp.float32)
            for j in range(1, terms.shape[1]):
                total += terms[slot, j, i].astype(jnp.float32)
            grads[i, pl.ds(slot * half_rows, half_rows), :] = total
        copy = pltpu.make_async_copy(grads.at[i], result, sems.at[i])
        copy.start()
        rows.append(copy)
    for copy in rows:
        copy.wait()


def shards(queries, key_states, value_states, out_grad, doc_ids):
    members = lax.axis_size("ctx")
    rows, width = queries.shape
    head_dim = key_states.shape[1]
    half_rows = rows // 2
    halo = -(-(members // 4) * half_rows // rows)
    groups = width // head_dim // GROUP_HEADS
    docs = doc_ids.reshape(doc_ids.shape[0] // LANES, LANES)
    vmem = pl.BlockSpec(memory_space=pltpu.VMEM)
    hbm = pl.BlockSpec(memory_space=pltpu.HBM)
    anywhere = pl.BlockSpec(memory_space=pl.ANY)
    dma = pltpu.SemaphoreType.DMA
    keys = (halo + 1) * rows
    group_shape = jax.ShapeDtypeStruct((groups, rows, GROUP_HEADS * head_dim), jnp.bfloat16)
    row_shape = jax.ShapeDtypeStruct((rows, width), jnp.bfloat16)
    grad_shape = jax.ShapeDtypeStruct((rows, head_dim), jnp.float32)
    operands = (queries, key_states, value_states, out_grad, docs)
    out_rows, dq_rows, terms = pl.pallas_call(
        functools.partial(kernel, members, halo),
        out_shape=(
            group_shape,
            group_shape,
            jax.ShapeDtypeStruct((2, halo + 1, 2, half_rows, head_dim), jnp.bfloat16),
        ),
        in_specs=[hbm] * 5,
        out_specs=(vmem, vmem, vmem),
        scratch_shapes=[
            pltpu.VMEM((rows, width), jnp.bfloat16),
            pltpu.VMEM((rows, head_dim), jnp.bfloat16),
            pltpu.VMEM((rows, head_dim), jnp.bfloat16),
            pltpu.VMEM((rows, width), jnp.bfloat16),
            pltpu.VMEM(docs.shape, jnp.int32),
            pltpu.VMEM((halo, 2, rows, head_dim), jnp.bfloat16),
            pltpu.VMEM(group_shape.shape, jnp.bfloat16),
            pltpu.VMEM(group_shape.shape, jnp.bfloat16),
            pltpu.VMEM((halo + 1, 2, 2, half_rows, head_dim), jnp.bfloat16),
            pltpu.VMEM((keys, width // head_dim * rows), jnp.float32),
            pltpu.VMEM((rows, width // head_dim * rows), jnp.float32),
            dma((5,)),
            dma((halo, 2)),
            dma((halo, 2)),
            dma((groups, 2, 2)),
            dma((groups, 2, 2)),
            dma((halo + 1, 2)),
            dma((2, halo + 1)),
        ],
        compiler_params=pltpu.CompilerParams(
            collective_id=0, has_side_effects=True, vmem_limit_bytes=40 * 1024 * 1024
        ),
        cost_estimate=pl.CostEstimate(
            flops=12 * rows * keys * width,
            bytes_accessed=8 * rows * width + 12 * rows * head_dim,
            transcendentals=rows * keys * width // head_dim,
        ),
    )(*(pltpu.with_memory_space_constraint(x, pltpu.HBM) for x in operands))
    return pl.pallas_call(
        finish,
        out_shape=(row_shape, row_shape, grad_shape, grad_shape),
        in_specs=[anywhere, anywhere, vmem],
        out_specs=(hbm,) * 4,
        scratch_shapes=[pltpu.VMEM((2, rows, head_dim), jnp.float32), dma((2, groups)), dma((2,))],
        compiler_params=pltpu.CompilerParams(vmem_limit_bytes=16 * 1024 * 1024),
    )(out_rows, dq_rows, terms)


def solution(mesh):
    placed = P(("grp", "ctx"), None)
    return jax.shard_map(
        shards,
        mesh=mesh,
        in_specs=(placed, placed, placed, placed, P("grp")),
        out_specs=(placed,) * 4,
        check_vma=False,
    )
```

```python
import functools
import math

import jax
import jax.numpy as jnp
from jax import lax
from jax.experimental import pallas as pl
from jax.experimental.pallas import tpu as pltpu
from jax.sharding import PartitionSpec as P

NEG_FILL = -1e30
LANES = 128
GROUP_HEADS = 2
MESH = pl.DeviceIdType.MESH


def dot(a, b, contract):
    return lax.dot_general(
        a, b, (((contract[0],), (contract[1],)), ((), ())), preferred_element_type=jnp.float32
    )


def kernel(
    members,
    span,
    q_hbm,
    k_hbm,
    v_hbm,
    g_hbm,
    doc_hbm,
    out_ref,
    dq_ref,
    own_terms,
    term_in,
    rows_in,
    window,
    doc_ref,
    doc_columns,
    bias,
    term_stage,
    load_sem,
    kv_send,
    kv_recv,
    relay_send,
    relay_recv,
    row_send,
    row_recv,
    term_send,
    term_recv,
):
    me = lax.axis_index("ctx")
    rows, width = q_hbm.shape
    head_dim = k_hbm.shape[1]
    size = rows // 2
    scaling = 1.0 / math.sqrt(head_dim)
    group_width = GROUP_HEADS * head_dim
    groups = width // group_width
    lanes = GROUP_HEADS * size
    keys = (span + 1) * size
    last = 2 * members - 1
    blocks = (me, last - me)

    def place(block):
        upper = block >= members
        return jnp.where(upper, last - block, block), upper.astype(jnp.int32)

    def remote(src, dst, send, recv, target):
        return pltpu.make_async_remote_copy(
            src_ref=src,
            dst_ref=dst,
            send_sem=send,
            recv_sem=recv,
            device_id={"ctx": target},
            device_id_type=MESH,
        )

    def flag(condition):
        return jnp.where(condition, 1, 0)

    def start(src, dst, send, recv, target, wanted=1):
        @pl.when(wanted * flag(target != me) == 1)
        def _():
            remote(src, dst, send, recv, target).start()

        @pl.when(wanted * flag(target == me) == 1)
        def _():
            pltpu.make_async_copy(src, dst, recv).start()

    def finish_send(src, dst, send, recv, target, wanted=1):
        @pl.when(wanted * flag(target != me) == 1)
        def _():
            remote(src, dst, send, recv, target).wait_send()

    def arrive(src, dst, recv):
        pltpu.make_async_copy(src, dst, recv).wait()

    barrier = pltpu.get_barrier_semaphore()

    def greet(device):
        pl.semaphore_signal(barrier, inc=1, device_id={"ctx": device}, device_id_type=MESH)

    expected = jnp.int32(0)
    for half in range(2):
        holder = blocks[half] // 2
        pl.when(holder != me)(functools.partial(greet, holder))
        target, _ = place(2 * me + half)
        expected += (target != me).astype(jnp.int32)
    for j in range(1, span + 1):
        pl.when(me - j >= 0)(functools.partial(greet, me - j))
        above, _ = place(me + j)
        pl.when(above != me)(functools.partial(greet, above))
        expected += (me - j >= 0).astype(jnp.int32) + (above != me).astype(jnp.int32)
    load = pltpu.make_async_copy(doc_hbm, doc_ref, load_sem)
    load.start()
    pl.semaphore_wait(barrier, expected)

    def kv_copy(i, half):
        target, slot = place(2 * me + half)
        return (
            (k_hbm, v_hbm)[i].at[pl.ds(half * size, size)],
            window.at[slot, span, i],
            kv_send.at[half, i],
            kv_recv.at[slot, i],
            target,
        )

    def row_copy(i, group, half):
        target, slot = place(2 * me + half)
        here = pl.ds(half * size, size)
        return (
            (q_hbm, g_hbm)[i].at[here, pl.ds(group * group_width, group_width)],
            rows_in.at[i, slot, group],
            row_send.at[i, half, group],
            row_recv.at[i, slot, group],
            target,
        )

    def relay_copy(slot, j):
        target, target_slot = place(blocks[slot] + j)
        return (
            window.at[slot, span],
            window.at[target_slot, span - j],
            relay_send.at[slot, j - 1],
            relay_recv.at[target_slot, j - 1],
            target,
        )

    def term_copy(slot, j):
        target, target_slot = place(blocks[slot] - j)
        return (
            term_stage.at[slot, j - 1],
            term_in.at[target_slot, j - 1],
            term_send.at[slot, j - 1],
            term_recv.at[target_slot, j - 1],
            target,
        )

    for half in range(2):
        for i in range(2):
            start(*kv_copy(i, half))
    for group in range(groups):
        for half in range(2):
            for i in range(2):
                start(*row_copy(i, group, half))

    load.wait()
    per_chunk = rows // LANES
    for slot, block in enumerate(blocks):
        chunk, odd = block // 2, block % 2
        row = jnp.concatenate(
            [doc_ref[pl.ds(chunk * per_chunk + i, 1), :] for i in range(per_chunk)], axis=1
        )
        turned = jnp.concatenate([row[:, size:], row[:, :size]], axis=1)
        query_doc = jnp.concatenate(
            [jnp.where(odd == 1, turned, row)[:, :size]] * GROUP_HEADS, axis=1
        )
        for back in range(span // 2, -1, -1):
            there = chunk - back
            for i in range(per_chunk):
                line = doc_ref[pl.ds(jnp.maximum(there, 0) * per_chunk + i, 1), :]
                column = jnp.broadcast_to(line, (LANES, LANES)).T
                low = ((span // 2 - back) * per_chunk + i) * LANES
                doc_columns[slot, low : low + LANES, :] = jnp.where(there >= 0, column, -1)
        key_doc = doc_columns[slot, pl.ds(pl.multiple_of(odd * size, size), keys), :]
        key_doc = jnp.concatenate([key_doc] * (lanes // LANES), axis=1)
        key_pos = lax.broadcasted_iota(jnp.int32, (keys, lanes), 0) - span * size
        query_pos = jnp.concatenate(
            [lax.broadcasted_iota(jnp.int32, (1, size), 1)] * GROUP_HEADS, axis=1
        )
        allowed = (key_doc == query_doc) & (key_pos <= query_pos)
        bias[slot] = jnp.where(allowed, 0.0, NEG_FILL)

    for slot, block in enumerate(blocks):
        for i, ref in enumerate((k_hbm, v_hbm)):
            arrive(ref.at[pl.ds(0, size)], window.at[slot, span, i], kv_recv.at[slot, i])
        for j in range(1, span + 1):
            start(*relay_copy(slot, j), flag(block + j <= last))

    for slot, block in enumerate(blocks):
        for j in range(1, span + 1):

            @pl.when(block - j >= 0)
            def _():
                arrive(
                    window.at[slot, span], window.at[slot, span - j], relay_recv.at[slot, j - 1]
                )

            @pl.when(block - j < 0)
            def _():
                window[slot, span - j] = jnp.zeros(window.shape[2:], window.dtype)

    totals = [(jnp.zeros((keys, head_dim), jnp.float32),) * 2 for _ in range(2)]

    def split(array):
        parts = [array[h * size : (h + 1) * size] for h in range(GROUP_HEADS)]
        return jnp.concatenate(parts, axis=1).astype(jnp.bfloat16)

    def stack(array):
        parts = [array[:, h * head_dim : (h + 1) * head_dim] for h in range(GROUP_HEADS)]
        return jnp.concatenate(parts, axis=0)

    for group in range(groups):
        at = pl.ds(group * group_width, group_width)
        for slot in range(2):
            for i, ref in enumerate((q_hbm, g_hbm)):
                arrive(
                    ref.at[pl.ds(0, size), at], rows_in.at[i, slot, group], row_recv.at[i, slot, group]
                )
        for slot in range(2):
            here = pl.ds(slot * size, size)
            key_win = jnp.concatenate([window[slot, p, 0] for p in range(span + 1)], axis=0)
            value_win = jnp.concatenate([window[slot, p, 1] for p in range(span + 1)], axis=0)
            query = stack(rows_in[0, slot, group])
            grad = stack(rows_in[1, slot, group])
            scores = dot(key_win, query, (1, 1)) + bias[slot]
            top = jnp.max(scores, axis=0, keepdims=True)
            raised = jnp.exp2((scores - top) * (scaling * math.log2(math.e)))
            weights = raised * (1.0 / jnp.sum(raised, axis=0, keepdims=True))
            probs = weights.astype(jnp.bfloat16)
            dprobs = dot(value_win, grad, (1, 1))
            row_dot = jnp.sum(weights * dprobs, axis=0, keepdims=True)
            dscores = (weights * (dprobs - row_dot)).astype(jnp.bfloat16)
            out_ref[here, at] = split(dot(probs, value_win, (0, 0)))
            dq_ref[here, at] = split(scaling * dot(dscores, key_win, (0, 0)))
            totals[slot] = (
                totals[slot][0] + dot(dscores, query, (1, 0)),
                totals[slot][1] + dot(probs, grad, (1, 0)),
            )

    for slot in range(2):
        for i, total in enumerate((totals[slot][0] * scaling, totals[slot][1])):
            own_terms[slot, i] = total[span * size :]
            for j in range(1, span + 1):
                low = (span - j) * size
                term_stage[slot, j - 1, i] = total[low : low + size].astype(jnp.bfloat16)
    for slot, block in enumerate(blocks):
        for j in range(1, span + 1):
            start(*term_copy(slot, j), flag(block - j >= 0))

    for half in range(2):
        for i in range(2):
            finish_send(*kv_copy(i, half))
            for group in range(groups):
                finish_send(*row_copy(i, group, half))
    for slot, block in enumerate(blocks):
        for j in range(1, span + 1):
            finish_send(*relay_copy(slot, j), flag(block + j <= last))

    for slot, block in enumerate(blocks):
        for j in range(1, span + 1):

            @pl.when(block + j <= last)
            def _():
                arrive(
                    term_stage.at[slot, j - 1], term_in.at[slot, j - 1], term_recv.at[slot, j - 1]
                )

            @pl.when(block + j > last)
            def _():
                term_in[slot, j - 1] = jnp.zeros(term_in.shape[2:], term_in.dtype)

    for slot, block in enumerate(blocks):
        for j in range(1, span + 1):
            finish_send(*term_copy(slot, j), flag(block - j >= 0))


def finish(out_in, dq_in, own_terms, terms, out_ref, dq_ref, dk_ref, dv_ref, grads, sems):
    copies = [
        pltpu.make_async_copy(out_in, out_ref, sems.at[0]),
        pltpu.make_async_copy(dq_in, dq_ref, sems.at[1]),
    ]
    for copy in copies:
        copy.start()
    size = terms.shape[3]
    for i, result in enumerate((dk_ref, dv_ref)):
        for slot in range(2):
            total = own_terms[slot, i]
            for j in range(terms.shape[1]):
                total += terms[slot, j, i].astype(jnp.float32)
            grads[i, pl.ds(slot * size, size), :] = total
        copy = pltpu.make_async_copy(grads.at[i], result, sems.at[2 + i])
        copy.start()
        copies.append(copy)
    for copy in copies:
        copy.wait()


def shards(queries, key_states, value_states, out_grad, doc_ids):
    members = lax.axis_size("ctx")
    rows, width = queries.shape
    head_dim = key_states.shape[1]
    size = rows // 2
    span = members // 4
    groups = width // head_dim // GROUP_HEADS
    keys = (span + 1) * size
    docs = doc_ids.reshape(doc_ids.shape[0] // LANES, LANES)
    vmem = pl.BlockSpec(memory_space=pltpu.VMEM)
    hbm = pl.BlockSpec(memory_space=pltpu.HBM)
    anywhere = pl.BlockSpec(memory_space=pl.ANY)
    dma = pltpu.SemaphoreType.DMA
    row_shape = jax.ShapeDtypeStruct((rows, width), jnp.bfloat16)
    grad_shape = jax.ShapeDtypeStruct((rows, head_dim), jnp.float32)
    operands = (queries, key_states, value_states, out_grad, docs)
    results = pl.pallas_call(
        functools.partial(kernel, members, span),
        out_shape=(
            row_shape,
            row_shape,
            jax.ShapeDtypeStruct((2, 2, size, head_dim), jnp.float32),
            jax.ShapeDtypeStruct((2, span, 2, size, head_dim), jnp.bfloat16),
        ),
        in_specs=[hbm] * 5,
        out_specs=(vmem,) * 4,
        scratch_shapes=[
            pltpu.VMEM((2, 2, groups, size, GROUP_HEADS * head_dim), jnp.bfloat16),
            pltpu.VMEM((2, span + 1, 2, size, head_dim), jnp.bfloat16),
            pltpu.VMEM(docs.shape, jnp.int32),
            pltpu.VMEM((2, (span + 2) * size, LANES), jnp.int32),
            pltpu.VMEM((2, keys, GROUP_HEADS * size), jnp.float32),
            pltpu.VMEM((2, span, 2, size, head_dim), jnp.bfloat16),
            dma,
            dma((2, 2)),
            dma((2, 2)),
            dma((2, span)),
            dma((2, span)),
            dma((2, 2, groups)),
            dma((2, 2, groups)),
            dma((2, span)),
            dma((2, span)),
        ],
        compiler_params=pltpu.CompilerParams(
            collective_id=0, has_side_effects=True, vmem_limit_bytes=40 * 1024 * 1024
        ),
        cost_estimate=pl.CostEstimate(
            flops=12 * rows * keys * width,
            bytes_accessed=8 * rows * width + 12 * rows * head_dim,
            transcendentals=rows * keys * width // head_dim,
        ),
    )(*(pltpu.with_memory_space_constraint(x, pltpu.HBM) for x in operands))
    return pl.pallas_call(
        finish,
        out_shape=(row_shape, row_shape, grad_shape, grad_shape),
        in_specs=[anywhere, anywhere, vmem, vmem],
        out_specs=(hbm,) * 4,
        scratch_shapes=[pltpu.VMEM((2, rows, head_dim), jnp.float32), dma((4,))],
        compiler_params=pltpu.CompilerParams(vmem_limit_bytes=16 * 1024 * 1024),
    )(*results)


def solution(mesh):
    placed = P(("grp", "ctx"), None)
    return jax.shard_map(
        shards,
        mesh=mesh,
        in_specs=(placed, placed, placed, placed, P("grp")),
        out_specs=(placed,) * 4,
        check_vma=False,
    )
```

```python
import functools
import math

import jax
import jax.numpy as jnp
from jax import lax
from jax.experimental import pallas as pl
from jax.experimental.pallas import tpu as pltpu
from jax.sharding import PartitionSpec as P

NEG_FILL = -1e30
LANES = 128
GROUP_HEADS = 2
MESH = pl.DeviceIdType.MESH


def dot(a, b, contract):
    return lax.dot_general(
        a, b, (((contract[0],), (contract[1],)), ((), ())), preferred_element_type=jnp.float32
    )


def kernel(
    members,
    span,
    q_hbm,
    k_hbm,
    v_hbm,
    g_hbm,
    doc_hbm,
    out_ref,
    dq_ref,
    own_terms,
    term_in,
    rows_in,
    window,
    doc_ref,
    doc_columns,
    bias,
    term_stage,
    load_sem,
    kv_send,
    kv_recv,
    relay_send,
    relay_recv,
    row_send,
    row_recv,
    term_send,
    term_recv,
):
    me = lax.axis_index("ctx")
    rows, width = q_hbm.shape
    head_dim = k_hbm.shape[1]
    size = rows // 2
    scaling = 1.0 / math.sqrt(head_dim)
    group_width = GROUP_HEADS * head_dim
    groups = width // group_width
    lanes = GROUP_HEADS * size
    keys = (span + 1) * size
    last = 2 * members - 1
    blocks = (me, last - me)

    def place(block):
        upper = block >= members
        return jnp.where(upper, last - block, block), upper.astype(jnp.int32)

    def remote(src, dst, send, recv, target):
        return pltpu.make_async_remote_copy(
            src_ref=src,
            dst_ref=dst,
            send_sem=send,
            recv_sem=recv,
            device_id={"ctx": target},
            device_id_type=MESH,
        )

    def flag(condition):
        return jnp.where(condition, 1, 0)

    def start(src, dst, send, recv, target, wanted=1):
        @pl.when(wanted * flag(target != me) == 1)
        def _():
            remote(src, dst, send, recv, target).start()

        @pl.when(wanted * flag(target == me) == 1)
        def _():
            pltpu.make_async_copy(src, dst, recv).start()

    def finish_send(src, dst, send, recv, target, wanted=1):
        @pl.when(wanted * flag(target != me) == 1)
        def _():
            remote(src, dst, send, recv, target).wait_send()

    def arrive(src, dst, recv):
        pltpu.make_async_copy(src, dst, recv).wait()

    barrier = pltpu.get_barrier_semaphore()

    def greet(device):
        pl.semaphore_signal(barrier, inc=1, device_id={"ctx": device}, device_id_type=MESH)

    expected = jnp.int32(0)
    for half in range(2):
        holder = blocks[half] // 2
        pl.when(holder != me)(functools.partial(greet, holder))
        target, _ = place(2 * me + half)
        expected += (target != me).astype(jnp.int32)
    for j in range(1, span + 1):
        pl.when(me - j >= 0)(functools.partial(greet, me - j))
        above, _ = place(me + j)
        pl.when(above != me)(functools.partial(greet, above))
        expected += (me - j >= 0).astype(jnp.int32) + (above != me).astype(jnp.int32)
    load = pltpu.make_async_copy(doc_hbm, doc_ref, load_sem)
    load.start()
    pl.semaphore_wait(barrier, expected)

    def kv_copy(i, half):
        target, slot = place(2 * me + half)
        return (
            (k_hbm, v_hbm)[i].at[pl.ds(half * size, size)],
            window.at[slot, span, i],
            kv_send.at[half, i],
            kv_recv.at[slot, i],
            target,
        )

    def row_copy(i, group, half):
        target, slot = place(2 * me + half)
        here = pl.ds(half * size, size)
        return (
            (q_hbm, g_hbm)[i].at[here, pl.ds(group * group_width, group_width)],
            rows_in.at[i, slot, group],
            row_send.at[i, half, group],
            row_recv.at[i, slot, group],
            target,
        )

    def relay_copy(slot, j):
        target, target_slot = place(blocks[slot] + j)
        return (
            window.at[slot, span],
            window.at[target_slot, span - j],
            relay_send.at[slot, j - 1],
            relay_recv.at[target_slot, j - 1],
            target,
        )

    def term_copy(slot, j):
        target, target_slot = place(blocks[slot] - j)
        return (
            term_stage.at[slot, j - 1],
            term_in.at[target_slot, j - 1],
            term_send.at[slot, j - 1],
            term_recv.at[target_slot, j - 1],
            target,
        )

    for half in range(2):
        for i in range(2):
            start(*kv_copy(i, half))

    def send_rows(group):
        for half in range(2):
            for i in range(2):
                start(*row_copy(i, group, half))

    send_rows(0)

    load.wait()
    per_chunk = rows // LANES
    for slot, block in enumerate(blocks):
        chunk, odd = block // 2, block % 2
        row = jnp.concatenate(
            [doc_ref[pl.ds(chunk * per_chunk + i, 1), :] for i in range(per_chunk)], axis=1
        )
        turned = jnp.concatenate([row[:, size:], row[:, :size]], axis=1)
        query_doc = jnp.concatenate(
            [jnp.where(odd == 1, turned, row)[:, :size]] * GROUP_HEADS, axis=1
        )
        for back in range(span // 2, -1, -1):
            there = chunk - back
            for i in range(per_chunk):
                line = doc_ref[pl.ds(jnp.maximum(there, 0) * per_chunk + i, 1), :]
                column = jnp.broadcast_to(line, (LANES, LANES)).T
                low = ((span // 2 - back) * per_chunk + i) * LANES
                doc_columns[slot, low : low + LANES, :] = jnp.where(there >= 0, column, -1)
        key_doc = doc_columns[slot, pl.ds(pl.multiple_of(odd * size, size), keys), :]
        key_doc = jnp.concatenate([key_doc] * (lanes // LANES), axis=1)
        key_pos = lax.broadcasted_iota(jnp.int32, (keys, lanes), 0) - span * size
        query_pos = jnp.concatenate(
            [lax.broadcasted_iota(jnp.int32, (1, size), 1)] * GROUP_HEADS, axis=1
        )
        allowed = (key_doc == query_doc) & (key_pos <= query_pos)
        bias[slot] = jnp.where(allowed, 0.0, NEG_FILL)

    for slot, block in enumerate(blocks):
        for i, ref in enumerate((k_hbm, v_hbm)):
            arrive(ref.at[pl.ds(0, size)], window.at[slot, span, i], kv_recv.at[slot, i])
        for j in range(1, span + 1):
            start(*relay_copy(slot, j), flag(block + j <= last))
    for group in range(1, groups):
        send_rows(group)

    for slot, block in enumerate(blocks):
        for j in range(1, span + 1):

            @pl.when(block - j >= 0)
            def _():
                arrive(
                    window.at[slot, span], window.at[slot, span - j], relay_recv.at[slot, j - 1]
                )

            @pl.when(block - j < 0)
            def _():
                window[slot, span - j] = jnp.zeros(window.shape[2:], window.dtype)

    totals = [(jnp.zeros((keys, head_dim), jnp.float32),) * 2 for _ in range(2)]

    def split(array):
        parts = [array[h * size : (h + 1) * size] for h in range(GROUP_HEADS)]
        return jnp.concatenate(parts, axis=1).astype(jnp.bfloat16)

    def stack(array):
        parts = [array[:, h * head_dim : (h + 1) * head_dim] for h in range(GROUP_HEADS)]
        return jnp.concatenate(parts, axis=0)

    for group in range(groups):
        at = pl.ds(group * group_width, group_width)
        for slot in range(2):
            for i, ref in enumerate((q_hbm, g_hbm)):
                arrive(
                    ref.at[pl.ds(0, size), at], rows_in.at[i, slot, group], row_recv.at[i, slot, group]
                )
        for slot in range(2):
            here = pl.ds(slot * size, size)
            key_win = jnp.concatenate([window[slot, p, 0] for p in range(span + 1)], axis=0)
            value_win = jnp.concatenate([window[slot, p, 1] for p in range(span + 1)], axis=0)
            query = stack(rows_in[0, slot, group])
            grad = stack(rows_in[1, slot, group])
            scores = dot(key_win, query, (1, 1)) + bias[slot]
            top = jnp.max(scores, axis=0, keepdims=True)
            raised = jnp.exp2((scores - top) * (scaling * math.log2(math.e)))
            weights = raised * (1.0 / jnp.sum(raised, axis=0, keepdims=True))
            probs = weights.astype(jnp.bfloat16)
            dprobs = dot(value_win, grad, (1, 1))
            row_dot = jnp.sum(weights * dprobs, axis=0, keepdims=True)
            dscores = (weights * (dprobs - row_dot)).astype(jnp.bfloat16)
            out_ref[here, at] = split(dot(probs, value_win, (0, 0)))
            dq_ref[here, at] = split(scaling * dot(dscores, key_win, (0, 0)))
            totals[slot] = (
                totals[slot][0] + dot(dscores, query, (1, 0)),
                totals[slot][1] + dot(probs, grad, (1, 0)),
            )

    for slot in range(2):
        for i, total in enumerate((totals[slot][0] * scaling, totals[slot][1])):
            own_terms[slot, i] = total[span * size :]
            for j in range(1, span + 1):
                low = (span - j) * size
                term_stage[slot, j - 1, i] = total[low : low + size].astype(jnp.bfloat16)
    for slot, block in enumerate(blocks):
        for j in range(1, span + 1):
            start(*term_copy(slot, j), flag(block - j >= 0))

    for half in range(2):
        for i in range(2):
            finish_send(*kv_copy(i, half))
            for group in range(groups):
                finish_send(*row_copy(i, group, half))
    for slot, block in enumerate(blocks):
        for j in range(1, span + 1):
            finish_send(*relay_copy(slot, j), flag(block + j <= last))

    for slot, block in enumerate(blocks):
        for j in range(1, span + 1):

            @pl.when(block + j <= last)
            def _():
                arrive(
                    term_stage.at[slot, j - 1], term_in.at[slot, j - 1], term_recv.at[slot, j - 1]
                )

            @pl.when(block + j > last)
            def _():
                term_in[slot, j - 1] = jnp.zeros(term_in.shape[2:], term_in.dtype)

    for slot, block in enumerate(blocks):
        for j in range(1, span + 1):
            finish_send(*term_copy(slot, j), flag(block - j >= 0))


def finish(out_in, dq_in, own_terms, terms, out_ref, dq_ref, dk_ref, dv_ref, grads, sems):
    copies = [
        pltpu.make_async_copy(out_in, out_ref, sems.at[0]),
        pltpu.make_async_copy(dq_in, dq_ref, sems.at[1]),
    ]
    for copy in copies:
        copy.start()
    size = terms.shape[3]
    for i, result in enumerate((dk_ref, dv_ref)):
        for slot in range(2):
            total = own_terms[slot, i]
            for j in range(terms.shape[1]):
                total += terms[slot, j, i].astype(jnp.float32)
            grads[i, pl.ds(slot * size, size), :] = total
        copy = pltpu.make_async_copy(grads.at[i], result, sems.at[2 + i])
        copy.start()
        copies.append(copy)
    for copy in copies:
        copy.wait()


def shards(queries, key_states, value_states, out_grad, doc_ids):
    members = lax.axis_size("ctx")
    rows, width = queries.shape
    head_dim = key_states.shape[1]
    size = rows // 2
    span = members // 4
    groups = width // head_dim // GROUP_HEADS
    keys = (span + 1) * size
    docs = doc_ids.reshape(doc_ids.shape[0] // LANES, LANES)
    vmem = pl.BlockSpec(memory_space=pltpu.VMEM)
    hbm = pl.BlockSpec(memory_space=pltpu.HBM)
    anywhere = pl.BlockSpec(memory_space=pl.ANY)
    dma = pltpu.SemaphoreType.DMA
    row_shape = jax.ShapeDtypeStruct((rows, width), jnp.bfloat16)
    grad_shape = jax.ShapeDtypeStruct((rows, head_dim), jnp.float32)
    operands = (queries, key_states, value_states, out_grad, docs)
    results = pl.pallas_call(
        functools.partial(kernel, members, span),
        out_shape=(
            row_shape,
            row_shape,
            jax.ShapeDtypeStruct((2, 2, size, head_dim), jnp.float32),
            jax.ShapeDtypeStruct((2, span, 2, size, head_dim), jnp.bfloat16),
        ),
        in_specs=[hbm] * 5,
        out_specs=(vmem,) * 4,
        scratch_shapes=[
            pltpu.VMEM((2, 2, groups, size, GROUP_HEADS * head_dim), jnp.bfloat16),
            pltpu.VMEM((2, span + 1, 2, size, head_dim), jnp.bfloat16),
            pltpu.VMEM(docs.shape, jnp.int32),
            pltpu.VMEM((2, (span + 2) * size, LANES), jnp.int32),
            pltpu.VMEM((2, keys, GROUP_HEADS * size), jnp.float32),
            pltpu.VMEM((2, span, 2, size, head_dim), jnp.bfloat16),
            dma,
            dma((2, 2)),
            dma((2, 2)),
            dma((2, span)),
            dma((2, span)),
            dma((2, 2, groups)),
            dma((2, 2, groups)),
            dma((2, span)),
            dma((2, span)),
        ],
        compiler_params=pltpu.CompilerParams(
            collective_id=0, has_side_effects=True, vmem_limit_bytes=40 * 1024 * 1024
        ),
        cost_estimate=pl.CostEstimate(
            flops=12 * rows * keys * width,
            bytes_accessed=8 * rows * width + 12 * rows * head_dim,
            transcendentals=rows * keys * width // head_dim,
        ),
    )(*(pltpu.with_memory_space_constraint(x, pltpu.HBM) for x in operands))
    return pl.pallas_call(
        finish,
        out_shape=(row_shape, row_shape, grad_shape, grad_shape),
        in_specs=[anywhere, anywhere, vmem, vmem],
        out_specs=(hbm,) * 4,
        scratch_shapes=[pltpu.VMEM((2, rows, head_dim), jnp.float32), dma((4,))],
        compiler_params=pltpu.CompilerParams(vmem_limit_bytes=16 * 1024 * 1024),
    )(*results)


def solution(mesh):
    placed = P(("grp", "ctx"), None)
    return jax.shard_map(
        shards,
        mesh=mesh,
        in_specs=(placed, placed, placed, placed, P("grp")),
        out_specs=(placed,) * 4,
        check_vma=False,
    )
```

```python
import functools
import math

import jax
import jax.numpy as jnp
from jax import lax
from jax.experimental import pallas as pl
from jax.experimental.pallas import tpu as pltpu
from jax.sharding import PartitionSpec as P

NEG_FILL = -1e30
LANES = 128
GROUP_HEADS = 2
MESH = pl.DeviceIdType.MESH


def dot(a, b, contract):
    return lax.dot_general(
        a, b, (((contract[0],), (contract[1],)), ((), ())), preferred_element_type=jnp.float32
    )


def kernel(
    members,
    span,
    q_hbm,
    k_hbm,
    v_hbm,
    g_hbm,
    doc_hbm,
    out_ref,
    dq_ref,
    own_terms,
    term_in,
    rows_in,
    window,
    doc_ref,
    doc_columns,
    bias,
    term_stage,
    load_sem,
    kv_send,
    kv_recv,
    relay_send,
    relay_recv,
    row_send,
    row_recv,
    term_send,
    term_recv,
):
    me = lax.axis_index("ctx")
    rows, width = q_hbm.shape
    head_dim = k_hbm.shape[1]
    size = rows // 2
    scaling = 1.0 / math.sqrt(head_dim)
    group_width = GROUP_HEADS * head_dim
    groups = width // group_width
    lanes = GROUP_HEADS * size
    keys = (span + 1) * size
    last = 2 * members - 1
    blocks = (me, last - me)

    def place(block):
        upper = block >= members
        return jnp.where(upper, last - block, block), upper.astype(jnp.int32)

    def remote(src, dst, send, recv, target):
        return pltpu.make_async_remote_copy(
            src_ref=src,
            dst_ref=dst,
            send_sem=send,
            recv_sem=recv,
            device_id={"ctx": target},
            device_id_type=MESH,
        )

    def flag(condition):
        return jnp.where(condition, 1, 0)

    def start(src, dst, send, recv, target, wanted=1):
        @pl.when(wanted * flag(target != me) == 1)
        def _():
            remote(src, dst, send, recv, target).start()

        @pl.when(wanted * flag(target == me) == 1)
        def _():
            pltpu.make_async_copy(src, dst, recv).start()

    def finish_send(src, dst, send, recv, target, wanted=1):
        @pl.when(wanted * flag(target != me) == 1)
        def _():
            remote(src, dst, send, recv, target).wait_send()

    def arrive(src, dst, recv):
        pltpu.make_async_copy(src, dst, recv).wait()

    barrier = pltpu.get_barrier_semaphore()

    def greet(device):
        pl.semaphore_signal(barrier, inc=1, device_id={"ctx": device}, device_id_type=MESH)

    expected = jnp.int32(0)
    for half in range(2):
        holder = blocks[half] // 2
        pl.when(holder != me)(functools.partial(greet, holder))
        target, _ = place(2 * me + half)
        expected += (target != me).astype(jnp.int32)
    for j in range(1, span + 1):
        pl.when(me - j >= 0)(functools.partial(greet, me - j))
        above, _ = place(me + j)
        pl.when(above != me)(functools.partial(greet, above))
        expected += (me - j >= 0).astype(jnp.int32) + (above != me).astype(jnp.int32)
    load = pltpu.make_async_copy(doc_hbm, doc_ref, load_sem)
    load.start()
    pl.semaphore_wait(barrier, expected)

    def kv_copy(i, half):
        target, slot = place(2 * me + half)
        return (
            (k_hbm, v_hbm)[i].at[pl.ds(half * size, size)],
            window.at[slot, span, i],
            kv_send.at[half, i],
            kv_recv.at[slot, i],
            target,
        )

    def row_copy(i, group, half):
        target, slot = place(2 * me + half)
        here = pl.ds(half * size, size)
        return (
            (q_hbm, g_hbm)[i].at[here, pl.ds(group * group_width, group_width)],
            rows_in.at[i, slot, group],
            row_send.at[i, half, group],
            row_recv.at[i, slot, group],
            target,
        )

    def relay_copy(slot, j):
        target, target_slot = place(blocks[slot] + j)
        return (
            window.at[slot, span],
            window.at[target_slot, span - j],
            relay_send.at[slot, j - 1],
            relay_recv.at[target_slot, j - 1],
            target,
        )

    def term_copy(slot, j):
        target, target_slot = place(blocks[slot] - j)
        return (
            term_stage.at[slot, j - 1],
            term_in.at[target_slot, j - 1],
            term_send.at[slot, j - 1],
            term_recv.at[target_slot, j - 1],
            target,
        )

    for half in range(2):
        for i in range(2):
            start(*kv_copy(i, half))

    def send_rows(group):
        for half in range(2):
            for i in range(2):
                start(*row_copy(i, group, half))

    send_rows(0)

    load.wait()
    per_chunk = rows // LANES
    for slot, block in enumerate(blocks):
        chunk, odd = block // 2, block % 2
        row = jnp.concatenate(
            [doc_ref[pl.ds(chunk * per_chunk + i, 1), :] for i in range(per_chunk)], axis=1
        )
        turned = jnp.concatenate([row[:, size:], row[:, :size]], axis=1)
        query_doc = jnp.concatenate(
            [jnp.where(odd == 1, turned, row)[:, :size]] * GROUP_HEADS, axis=1
        )
        for back in range(span // 2, -1, -1):
            there = chunk - back
            for i in range(per_chunk):
                line = doc_ref[pl.ds(jnp.maximum(there, 0) * per_chunk + i, 1), :]
                column = jnp.broadcast_to(line, (LANES, LANES)).T
                low = ((span // 2 - back) * per_chunk + i) * LANES
                doc_columns[slot, low : low + LANES, :] = jnp.where(there >= 0, column, -1)
        key_doc = doc_columns[slot, pl.ds(pl.multiple_of(odd * size, size), keys), :]
        key_doc = jnp.concatenate([key_doc] * (lanes // LANES), axis=1)
        key_pos = lax.broadcasted_iota(jnp.int32, (keys, lanes), 0) - span * size
        query_pos = jnp.concatenate(
            [lax.broadcasted_iota(jnp.int32, (1, size), 1)] * GROUP_HEADS, axis=1
        )
        allowed = (key_doc == query_doc) & (key_pos <= query_pos)
        bias[slot] = jnp.where(allowed, 0.0, NEG_FILL)

    for slot, block in enumerate(blocks):
        for i, ref in enumerate((k_hbm, v_hbm)):
            arrive(ref.at[pl.ds(0, size)], window.at[slot, span, i], kv_recv.at[slot, i])
        for j in range(1, span + 1):
            start(*relay_copy(slot, j), flag(block + j <= last))
    for group in range(1, groups):
        send_rows(group)

    for slot, block in enumerate(blocks):
        for j in range(1, span + 1):

            @pl.when(block - j >= 0)
            def _():
                arrive(
                    window.at[slot, span], window.at[slot, span - j], relay_recv.at[slot, j - 1]
                )

            @pl.when(block - j < 0)
            def _():
                window[slot, span - j] = jnp.zeros(window.shape[2:], window.dtype)

    totals = [(jnp.zeros((keys, head_dim), jnp.float32),) * 2 for _ in range(2)]

    def split(array):
        parts = [array[h * size : (h + 1) * size] for h in range(GROUP_HEADS)]
        return jnp.concatenate(parts, axis=1).astype(jnp.bfloat16)

    def stack(array):
        parts = [array[:, h * head_dim : (h + 1) * head_dim] for h in range(GROUP_HEADS)]
        return jnp.concatenate(parts, axis=0)

    def send_terms(slot):
        for i, total in enumerate((totals[slot][0] * scaling, totals[slot][1])):
            own_terms[slot, i] = total[span * size :]
            for j in range(1, span + 1):
                low = (span - j) * size
                term_stage[slot, j - 1, i] = total[low : low + size].astype(jnp.bfloat16)
        for j in range(1, span + 1):
            start(*term_copy(slot, j), flag(blocks[slot] - j >= 0))

    def windows(slot):
        return [
            jnp.concatenate([window[slot, p, i] for p in range(span + 1)], axis=0)
            for i in range(2)
        ]

    def write_rows(group, slot, probs, dscores):
        here = pl.ds(slot * size, size)
        at = pl.ds(group * group_width, group_width)
        key_win, value_win = windows(slot)
        out_ref[here, at] = split(dot(probs, value_win, (0, 0)))
        dq_ref[here, at] = split(scaling * dot(dscores, key_win, (0, 0)))

    for group in range(groups):
        at = pl.ds(group * group_width, group_width)
        later = []
        for slot in range(2):
            for i, ref in enumerate((q_hbm, g_hbm)):
                arrive(
                    ref.at[pl.ds(0, size), at], rows_in.at[i, slot, group], row_recv.at[i, slot, group]
                )
            key_win, value_win = windows(slot)
            query = stack(rows_in[0, slot, group])
            grad = stack(rows_in[1, slot, group])
            scores = dot(key_win, query, (1, 1)) + bias[slot]
            top = jnp.max(scores, axis=0, keepdims=True)
            raised = jnp.exp2((scores - top) * (scaling * math.log2(math.e)))
            weights = raised * (1.0 / jnp.sum(raised, axis=0, keepdims=True))
            probs = weights.astype(jnp.bfloat16)
            dprobs = dot(value_win, grad, (1, 1))
            row_dot = jnp.sum(weights * dprobs, axis=0, keepdims=True)
            dscores = (weights * (dprobs - row_dot)).astype(jnp.bfloat16)
            totals[slot] = (
                totals[slot][0] + dot(dscores, query, (1, 0)),
                totals[slot][1] + dot(probs, grad, (1, 0)),
            )
            if group < groups - 1:
                write_rows(group, slot, probs, dscores)
            else:
                send_terms(slot)
                later.append((probs, dscores))
        for slot, kept in enumerate(later):
            write_rows(group, slot, *kept)

    for half in range(2):
        for i in range(2):
            finish_send(*kv_copy(i, half))
            for group in range(groups):
                finish_send(*row_copy(i, group, half))
    for slot, block in enumerate(blocks):
        for j in range(1, span + 1):
            finish_send(*relay_copy(slot, j), flag(block + j <= last))

    for slot, block in enumerate(blocks):
        for j in range(1, span + 1):

            @pl.when(block + j <= last)
            def _():
                arrive(
                    term_stage.at[slot, j - 1], term_in.at[slot, j - 1], term_recv.at[slot, j - 1]
                )

            @pl.when(block + j > last)
            def _():
                term_in[slot, j - 1] = jnp.zeros(term_in.shape[2:], term_in.dtype)

    for slot, block in enumerate(blocks):
        for j in range(1, span + 1):
            finish_send(*term_copy(slot, j), flag(block - j >= 0))


def finish(out_in, dq_in, own_terms, terms, out_ref, dq_ref, dk_ref, dv_ref, grads, sems):
    copies = [
        pltpu.make_async_copy(out_in, out_ref, sems.at[0]),
        pltpu.make_async_copy(dq_in, dq_ref, sems.at[1]),
    ]
    for copy in copies:
        copy.start()
    size = terms.shape[3]
    for i, result in enumerate((dk_ref, dv_ref)):
        for slot in range(2):
            total = own_terms[slot, i]
            for j in range(terms.shape[1]):
                total += terms[slot, j, i].astype(jnp.float32)
            grads[i, pl.ds(slot * size, size), :] = total
        copy = pltpu.make_async_copy(grads.at[i], result, sems.at[2 + i])
        copy.start()
        copies.append(copy)
    for copy in copies:
        copy.wait()


def shards(queries, key_states, value_states, out_grad, doc_ids):
    members = lax.axis_size("ctx")
    rows, width = queries.shape
    head_dim = key_states.shape[1]
    size = rows // 2
    span = members // 4
    groups = width // head_dim // GROUP_HEADS
    keys = (span + 1) * size
    docs = doc_ids.reshape(doc_ids.shape[0] // LANES, LANES)
    vmem = pl.BlockSpec(memory_space=pltpu.VMEM)
    hbm = pl.BlockSpec(memory_space=pltpu.HBM)
    anywhere = pl.BlockSpec(memory_space=pl.ANY)
    dma = pltpu.SemaphoreType.DMA
    row_shape = jax.ShapeDtypeStruct((rows, width), jnp.bfloat16)
    grad_shape = jax.ShapeDtypeStruct((rows, head_dim), jnp.float32)
    operands = (queries, key_states, value_states, out_grad, docs)
    results = pl.pallas_call(
        functools.partial(kernel, members, span),
        out_shape=(
            row_shape,
            row_shape,
            jax.ShapeDtypeStruct((2, 2, size, head_dim), jnp.float32),
            jax.ShapeDtypeStruct((2, span, 2, size, head_dim), jnp.bfloat16),
        ),
        in_specs=[hbm] * 5,
        out_specs=(vmem,) * 4,
        scratch_shapes=[
            pltpu.VMEM((2, 2, groups, size, GROUP_HEADS * head_dim), jnp.bfloat16),
            pltpu.VMEM((2, span + 1, 2, size, head_dim), jnp.bfloat16),
            pltpu.VMEM(docs.shape, jnp.int32),
            pltpu.VMEM((2, (span + 2) * size, LANES), jnp.int32),
            pltpu.VMEM((2, keys, GROUP_HEADS * size), jnp.float32),
            pltpu.VMEM((2, span, 2, size, head_dim), jnp.bfloat16),
            dma,
            dma((2, 2)),
            dma((2, 2)),
            dma((2, span)),
            dma((2, span)),
            dma((2, 2, groups)),
            dma((2, 2, groups)),
            dma((2, span)),
            dma((2, span)),
        ],
        compiler_params=pltpu.CompilerParams(
            collective_id=0, has_side_effects=True, vmem_limit_bytes=40 * 1024 * 1024
        ),
        cost_estimate=pl.CostEstimate(
            flops=12 * rows * keys * width,
            bytes_accessed=8 * rows * width + 12 * rows * head_dim,
            transcendentals=rows * keys * width // head_dim,
        ),
    )(*(pltpu.with_memory_space_constraint(x, pltpu.HBM) for x in operands))
    return pl.pallas_call(
        finish,
        out_shape=(row_shape, row_shape, grad_shape, grad_shape),
        in_specs=[anywhere, anywhere, vmem, vmem],
        out_specs=(hbm,) * 4,
        scratch_shapes=[pltpu.VMEM((2, rows, head_dim), jnp.float32), dma((4,))],
        compiler_params=pltpu.CompilerParams(vmem_limit_bytes=16 * 1024 * 1024),
    )(*results)


def solution(mesh):
    placed = P(("grp", "ctx"), None)
    return jax.shard_map(
        shards,
        mesh=mesh,
        in_specs=(placed, placed, placed, placed, P("grp")),
        out_specs=(placed,) * 4,
        check_vma=False,
    )
```

```python
import functools
import math

import jax
import jax.numpy as jnp
from jax import lax
from jax.experimental import pallas as pl
from jax.experimental.pallas import tpu as pltpu
from jax.sharding import PartitionSpec as P

NEG_FILL = -1e30
LANES = 128
GROUP_HEADS = 2
MESH = pl.DeviceIdType.MESH


def dot(a, b, contract):
    return lax.dot_general(
        a, b, (((contract[0],), (contract[1],)), ((), ())), preferred_element_type=jnp.float32
    )


def kernel(
    members,
    span,
    q_hbm,
    k_hbm,
    v_hbm,
    g_hbm,
    doc_hbm,
    out_ref,
    dq_ref,
    own_terms,
    term_in,
    rows_in,
    window,
    doc_ref,
    doc_columns,
    bias,
    term_stage,
    load_sem,
    kv_send,
    kv_recv,
    relay_send,
    relay_recv,
    row_send,
    row_recv,
    term_send,
    term_recv,
):
    me = lax.axis_index("ctx")
    rows, width = q_hbm.shape
    head_dim = k_hbm.shape[1]
    size = rows // 2
    scaling = 1.0 / math.sqrt(head_dim)
    group_width = GROUP_HEADS * head_dim
    groups = width // group_width
    lanes = GROUP_HEADS * size
    keys = (span + 1) * size
    last = 2 * members - 1
    blocks = (me, last - me)

    def place(block):
        upper = block >= members
        return jnp.where(upper, last - block, block), upper.astype(jnp.int32)

    def remote(src, dst, send, recv, target):
        return pltpu.make_async_remote_copy(
            src_ref=src,
            dst_ref=dst,
            send_sem=send,
            recv_sem=recv,
            device_id={"ctx": target},
            device_id_type=MESH,
        )

    def flag(condition):
        return jnp.where(condition, 1, 0)

    def start(src, dst, send, recv, target, wanted=1):
        @pl.when(wanted * flag(target != me) == 1)
        def _():
            remote(src, dst, send, recv, target).start()

        @pl.when(wanted * flag(target == me) == 1)
        def _():
            pltpu.make_async_copy(src, dst, recv).start()

    def finish_send(src, dst, send, recv, target, wanted=1):
        @pl.when(wanted * flag(target != me) == 1)
        def _():
            remote(src, dst, send, recv, target).wait_send()

    def arrive(src, dst, recv):
        pltpu.make_async_copy(src, dst, recv).wait()

    barrier = pltpu.get_barrier_semaphore()

    def greet(device):
        pl.semaphore_signal(barrier, inc=1, device_id={"ctx": device}, device_id_type=MESH)

    expected = jnp.int32(0)
    for half in range(2):
        holder = blocks[half] // 2
        pl.when(holder != me)(functools.partial(greet, holder))
        target, _ = place(2 * me + half)
        expected += (target != me).astype(jnp.int32)
    for j in range(1, span + 1):
        pl.when(me - j >= 0)(functools.partial(greet, me - j))
        above, _ = place(me + j)
        pl.when(above != me)(functools.partial(greet, above))
        expected += (me - j >= 0).astype(jnp.int32) + (above != me).astype(jnp.int32)
    load = pltpu.make_async_copy(doc_hbm, doc_ref, load_sem)
    load.start()
    pl.semaphore_wait(barrier, expected)

    def kv_copy(i, half):
        target, slot = place(2 * me + half)
        return (
            (k_hbm, v_hbm)[i].at[pl.ds(half * size, size)],
            window.at[slot, span, i],
            kv_send.at[half, i],
            kv_recv.at[slot, i],
            target,
        )

    def row_copy(i, group, half):
        target, slot = place(2 * me + half)
        here = pl.ds(half * size, size)
        return (
            (q_hbm, g_hbm)[i].at[here, pl.ds(group * group_width, group_width)],
            rows_in.at[i, slot, group],
            row_send.at[i, half, group],
            row_recv.at[i, slot, group],
            target,
        )

    def relay_copy(slot, j):
        target, target_slot = place(blocks[slot] + j)
        return (
            window.at[slot, span],
            window.at[target_slot, span - j],
            relay_send.at[slot, j - 1],
            relay_recv.at[target_slot, j - 1],
            target,
        )

    def term_copy(slot, j):
        target, target_slot = place(blocks[slot] - j)
        return (
            term_stage.at[slot, j - 1],
            term_in.at[target_slot, j - 1],
            term_send.at[slot, j - 1],
            term_recv.at[target_slot, j - 1],
            target,
        )

    for half in range(2):
        for i in range(2):
            start(*kv_copy(i, half))

    def send_rows(group):
        for half in range(2):
            for i in range(2):
                start(*row_copy(i, group, half))

    send_rows(0)
    send_rows(1)

    load.wait()
    per_chunk = rows // LANES
    for slot, block in enumerate(blocks):
        chunk, odd = block // 2, block % 2
        row = jnp.concatenate(
            [doc_ref[pl.ds(chunk * per_chunk + i, 1), :] for i in range(per_chunk)], axis=1
        )
        turned = jnp.concatenate([row[:, size:], row[:, :size]], axis=1)
        query_doc = jnp.concatenate(
            [jnp.where(odd == 1, turned, row)[:, :size]] * GROUP_HEADS, axis=1
        )
        for back in range(span // 2, -1, -1):
            there = chunk - back
            for i in range(per_chunk):
                line = doc_ref[pl.ds(jnp.maximum(there, 0) * per_chunk + i, 1), :]
                column = jnp.broadcast_to(line, (LANES, LANES)).T
                low = ((span // 2 - back) * per_chunk + i) * LANES
                doc_columns[slot, low : low + LANES, :] = jnp.where(there >= 0, column, -1)
        key_doc = doc_columns[slot, pl.ds(pl.multiple_of(odd * size, size), keys), :]
        key_doc = jnp.concatenate([key_doc] * (lanes // LANES), axis=1)
        key_pos = lax.broadcasted_iota(jnp.int32, (keys, lanes), 0) - span * size
        query_pos = jnp.concatenate(
            [lax.broadcasted_iota(jnp.int32, (1, size), 1)] * GROUP_HEADS, axis=1
        )
        allowed = (key_doc == query_doc) & (key_pos <= query_pos)
        bias[slot] = jnp.where(allowed, 0.0, NEG_FILL)

    for slot, block in enumerate(blocks):
        for i, ref in enumerate((k_hbm, v_hbm)):
            arrive(ref.at[pl.ds(0, size)], window.at[slot, span, i], kv_recv.at[slot, i])
        for j in range(1, span + 1):
            start(*relay_copy(slot, j), flag(block + j <= last))
    for group in range(2, groups):
        send_rows(group)

    for slot, block in enumerate(blocks):
        for j in range(1, span + 1):

            @pl.when(block - j >= 0)
            def _():
                arrive(
                    window.at[slot, span], window.at[slot, span - j], relay_recv.at[slot, j - 1]
                )

            @pl.when(block - j < 0)
            def _():
                window[slot, span - j] = jnp.zeros(window.shape[2:], window.dtype)

    totals = [(jnp.zeros((keys, head_dim), jnp.float32),) * 2 for _ in range(2)]

    def split(array):
        parts = [array[h * size : (h + 1) * size] for h in range(GROUP_HEADS)]
        return jnp.concatenate(parts, axis=1).astype(jnp.bfloat16)

    def stack(array):
        parts = [array[:, h * head_dim : (h + 1) * head_dim] for h in range(GROUP_HEADS)]
        return jnp.concatenate(parts, axis=0)

    def send_terms(slot):
        for i, total in enumerate((totals[slot][0] * scaling, totals[slot][1])):
            own_terms[slot, i] = total[span * size :]
            for j in range(1, span + 1):
                low = (span - j) * size
                term_stage[slot, j - 1, i] = total[low : low + size].astype(jnp.bfloat16)
        for j in range(1, span + 1):
            start(*term_copy(slot, j), flag(blocks[slot] - j >= 0))

    def windows(slot):
        return [
            jnp.concatenate([window[slot, p, i] for p in range(span + 1)], axis=0)
            for i in range(2)
        ]

    def write_rows(group, slot, probs, dscores):
        here = pl.ds(slot * size, size)
        at = pl.ds(group * group_width, group_width)
        key_win, value_win = windows(slot)
        out_ref[here, at] = split(dot(probs, value_win, (0, 0)))
        dq_ref[here, at] = split(scaling * dot(dscores, key_win, (0, 0)))

    for group in range(groups):
        at = pl.ds(group * group_width, group_width)
        later = []
        for slot in range(2):
            for i, ref in enumerate((q_hbm, g_hbm)):
                arrive(
                    ref.at[pl.ds(0, size), at], rows_in.at[i, slot, group], row_recv.at[i, slot, group]
                )
            key_win, value_win = windows(slot)
            query = stack(rows_in[0, slot, group])
            grad = stack(rows_in[1, slot, group])
            scores = dot(key_win, query, (1, 1)) + bias[slot]
            top = jnp.max(scores, axis=0, keepdims=True)
            raised = jnp.exp2((scores - top) * (scaling * math.log2(math.e)))
            weights = raised * (1.0 / jnp.sum(raised, axis=0, keepdims=True))
            probs = weights.astype(jnp.bfloat16)
            dprobs = dot(value_win, grad, (1, 1))
            row_dot = jnp.sum(weights * dprobs, axis=0, keepdims=True)
            dscores = (weights * (dprobs - row_dot)).astype(jnp.bfloat16)
            totals[slot] = (
                totals[slot][0] + dot(dscores, query, (1, 0)),
                totals[slot][1] + dot(probs, grad, (1, 0)),
            )
            if group < groups - 1:
                write_rows(group, slot, probs, dscores)
            else:
                send_terms(slot)
                later.append((probs, dscores))
        for slot, kept in enumerate(later):
            write_rows(group, slot, *kept)

    for half in range(2):
        for i in range(2):
            finish_send(*kv_copy(i, half))
            for group in range(groups):
                finish_send(*row_copy(i, group, half))
    for slot, block in enumerate(blocks):
        for j in range(1, span + 1):
            finish_send(*relay_copy(slot, j), flag(block + j <= last))

    for slot, block in enumerate(blocks):
        for j in range(1, span + 1):

            @pl.when(block + j <= last)
            def _():
                arrive(
                    term_stage.at[slot, j - 1], term_in.at[slot, j - 1], term_recv.at[slot, j - 1]
                )

            @pl.when(block + j > last)
            def _():
                term_in[slot, j - 1] = jnp.zeros(term_in.shape[2:], term_in.dtype)

    for slot, block in enumerate(blocks):
        for j in range(1, span + 1):
            finish_send(*term_copy(slot, j), flag(block - j >= 0))


def finish(out_in, dq_in, own_terms, terms, out_ref, dq_ref, dk_ref, dv_ref, grads, sems):
    copies = [
        pltpu.make_async_copy(out_in, out_ref, sems.at[0]),
        pltpu.make_async_copy(dq_in, dq_ref, sems.at[1]),
    ]
    for copy in copies:
        copy.start()
    size = terms.shape[3]
    for i, result in enumerate((dk_ref, dv_ref)):
        for slot in range(2):
            total = own_terms[slot, i]
            for j in range(terms.shape[1]):
                total += terms[slot, j, i].astype(jnp.float32)
            grads[i, pl.ds(slot * size, size), :] = total
        copy = pltpu.make_async_copy(grads.at[i], result, sems.at[2 + i])
        copy.start()
        copies.append(copy)
    for copy in copies:
        copy.wait()


def shards(queries, key_states, value_states, out_grad, doc_ids):
    members = lax.axis_size("ctx")
    rows, width = queries.shape
    head_dim = key_states.shape[1]
    size = rows // 2
    span = members // 4
    groups = width // head_dim // GROUP_HEADS
    keys = (span + 1) * size
    docs = doc_ids.reshape(doc_ids.shape[0] // LANES, LANES)
    vmem = pl.BlockSpec(memory_space=pltpu.VMEM)
    hbm = pl.BlockSpec(memory_space=pltpu.HBM)
    anywhere = pl.BlockSpec(memory_space=pl.ANY)
    dma = pltpu.SemaphoreType.DMA
    row_shape = jax.ShapeDtypeStruct((rows, width), jnp.bfloat16)
    grad_shape = jax.ShapeDtypeStruct((rows, head_dim), jnp.float32)
    operands = (queries, key_states, value_states, out_grad, docs)
    results = pl.pallas_call(
        functools.partial(kernel, members, span),
        out_shape=(
            row_shape,
            row_shape,
            jax.ShapeDtypeStruct((2, 2, size, head_dim), jnp.float32),
            jax.ShapeDtypeStruct((2, span, 2, size, head_dim), jnp.bfloat16),
        ),
        in_specs=[hbm] * 5,
        out_specs=(vmem,) * 4,
        scratch_shapes=[
            pltpu.VMEM((2, 2, groups, size, GROUP_HEADS * head_dim), jnp.bfloat16),
            pltpu.VMEM((2, span + 1, 2, size, head_dim), jnp.bfloat16),
            pltpu.VMEM(docs.shape, jnp.int32),
            pltpu.VMEM((2, (span + 2) * size, LANES), jnp.int32),
            pltpu.VMEM((2, keys, GROUP_HEADS * size), jnp.float32),
            pltpu.VMEM((2, span, 2, size, head_dim), jnp.bfloat16),
            dma,
            dma((2, 2)),
            dma((2, 2)),
            dma((2, span)),
            dma((2, span)),
            dma((2, 2, groups)),
            dma((2, 2, groups)),
            dma((2, span)),
            dma((2, span)),
        ],
        compiler_params=pltpu.CompilerParams(
            collective_id=0, has_side_effects=True, vmem_limit_bytes=40 * 1024 * 1024
        ),
        cost_estimate=pl.CostEstimate(
            flops=12 * rows * keys * width,
            bytes_accessed=8 * rows * width + 12 * rows * head_dim,
            transcendentals=rows * keys * width // head_dim,
        ),
    )(*(pltpu.with_memory_space_constraint(x, pltpu.HBM) for x in operands))
    return pl.pallas_call(
        finish,
        out_shape=(row_shape, row_shape, grad_shape, grad_shape),
        in_specs=[anywhere, anywhere, vmem, vmem],
        out_specs=(hbm,) * 4,
        scratch_shapes=[pltpu.VMEM((2, rows, head_dim), jnp.float32), dma((4,))],
        compiler_params=pltpu.CompilerParams(vmem_limit_bytes=16 * 1024 * 1024),
    )(*results)


def solution(mesh):
    placed = P(("grp", "ctx"), None)
    return jax.shard_map(
        shards,
        mesh=mesh,
        in_specs=(placed, placed, placed, placed, P("grp")),
        out_specs=(placed,) * 4,
        check_vma=False,
    )
```
